128 devices in a mesh: dp: 4 (over x), pipe: 2 (over z_hi), tensor: 16 (over z_lo, y, core).
Axes of the slice: x: 4, y: 4, z: 4 (z_hi: 2, z_lo: 2; z = z_hi * 2 + z_lo), core: 2. Of those that a mesh axis runs over, the one named last changes fastest.
Arguments:
- activations: bfloat16 [4, 256, 12288], P(None, 'dp', 'tensor'), may hold values from -40 to 40
- gains: float32 [2, 12288], P('pipe', 'tensor'), may hold values from 0.1 to 1.9
- block_values: bfloat16 [2, 192, 48, 4096], P('pipe', 'tensor'), may hold values from -0.109375 to 0.109375
- block_rows: int32 [2, 192, 48], P('pipe', 'tensor'), may hold values from 0 to 191, as said below
Outputs:
- hessians: float32 [2, 12288, 12288], P('pipe', 'dp', 'tensor')
- sections: bfloat16 [2, 4, 256, 12288], P('pipe', None, 'dp', 'tensor')
The draws below stay inside these ranges and needn't reach their ends.
Inputs may be any that keep to these rules, and one draw needn't show every extreme that they name: `block_rows`: for each section and column block the 48 row-block numbers are distinct.
All inputs are finite; a program needn't handle non-finite values.
Results may differ from the reference program's by a relative error of at most 0.009.
Values may be sent and summed in bfloat16 or wider, within the bound.
No kernel may reach another device: no remote copies, remote signals or barrier semaphores. Data moves between devices by JAX's collectives and lax.ppermute only.
A program may use at most 192 MiB of HBM per device.

```python
import jax
import jax.numpy as jnp
from jax import lax

D = 12288
BLOCK = 64
KEEP = 48
M = 4
SECTIONS = 2
BATCH = 256
NBC = 192


def draw_activations(key, part):
    key = jax.random.fold_in(key, 3)
    first, second, third = jax.random.split(key, 3)
    columns = jnp.arange(D, dtype=jnp.float32)
    col_scale = jnp.exp(0.55 * (2.0 * columns / (D - 1) - 1.0)) * jnp.exp(jax.random.uniform(second, (D,), jnp.float32, -0.6, 0.6))
    row_scale = jnp.exp(jax.random.uniform(third, (M, BATCH, 1), jnp.float32, -1.15, 1.15))
    noise = jax.random.normal(first, (M, BATCH, D), jnp.float32)
    noise = jnp.clip(noise, -4.0, 4.0)
    return (noise * col_scale * row_scale).astype(jnp.bfloat16)


def draw_block_rows(key, part):
    key = jax.random.fold_in(key, 7)
    keys = jax.random.split(key, SECTIONS * NBC)

    def pick(single):
        return jax.random.permutation(single, D // BLOCK)[:KEEP]
    chosen = jax.vmap(pick)(keys)
    return chosen.reshape(SECTIONS, NBC, KEEP).astype(jnp.int32)


def steps_of(key, dims, shards, least, largest):
    level, own = 1.0, jax.random.fold_in(key, 6)
    for axis_at, blocks in shards:
        heights = jnp.exp(jax.random.uniform(jax.random.fold_in(own, axis_at), (blocks,), jnp.float32, least / len(shards), largest / len(shards)))
        level = level * jnp.repeat(heights, dims[axis_at] // blocks).reshape([-1 if axis == axis_at else 1 for axis in range(len(dims))])
    return level


def centred(own_key, dims, spread, reach, shards=(), kind=jnp.bfloat16):
    result = jax.random.normal(own_key, dims, jnp.float32) * spread
    if len(shards) > 0:
        result = steps_of(own_key, dims, shards, -0.22, 0.18) * result
    return jnp.clip(result, min=-reach, max=reach).astype(kind)


def setup_inputs(seed: int = 0) -> dict:
    key_list = jax.random.split(jax.random.key(seed), 5)
    return {
        "activations": draw_activations(jax.random.fold_in(key_list[4], 71), 0),
        "gains": jnp.clip(1.0 + 0.18 * jax.random.normal(key_list[1], (SECTIONS, D), jnp.float32), 0.1, 1.9),
        "block_values": centred(key_list[2], (SECTIONS, NBC, KEEP, BLOCK * BLOCK), (KEEP * BLOCK) ** -0.5, 0.109375, ((0, 2), (1, 16))),
        "block_rows": draw_block_rows(jax.random.fold_in(key_list[4], 71), 0),
    }


epsilon_value = 1e-05

def layer_norm(stream, gain):
    values = stream.astype(jnp.float32)
    mean = lax.optimization_barrier(jnp.mean(values, axis=1, keepdims=True))
    square = lax.optimization_barrier(jnp.mean(values * values, axis=1, keepdims=True))
    scaled = (values - mean) * lax.rsqrt(square - mean * mean + epsilon_value)
    return (scaled * gain[None, :].astype(jnp.float32)).astype(jnp.bfloat16)

def sparse_product(normed, values, rows_index):
    count = normed.shape[0]
    view = normed.reshape(count, D // BLOCK, BLOCK)

    def one_block(item):
        tile, picks = item
        chosen = jnp.take(view, picks.astype(jnp.int32), axis=1).reshape(count, KEEP * BLOCK)
        return jnp.dot(chosen, tile.reshape(KEEP * BLOCK, BLOCK), preferred_element_type=jnp.float32)
    columns = lax.map(one_block, (values, rows_index))
    return jnp.transpose(columns, (1, 0, 2)).reshape(count, D)

def reference(activations, gains, block_values, block_rows):
    stream = activations.reshape(M * BATCH, D)
    hessian_list = []
    section_list = []
    for section in range(SECTIONS):
        normed = layer_norm(stream, gains[section])
        update = sparse_product(normed, block_values[section], block_rows[section])
        stream = (stream.astype(jnp.float32) + update).astype(jnp.bfloat16)
        section_list.append(stream.reshape(M, BATCH, D))
        gram = jnp.dot(normed.T, normed, preferred_element_type=jnp.float32)
        hessian_list.append(gram * (2.0 / (M * BATCH)))
    return (jnp.stack(hessian_list), jnp.stack(section_list))
```

```python
import functools

import jax
import jax.numpy as jnp
from jax import lax
from jax.experimental import pallas as pl
from jax.experimental.pallas import tpu as pltpu
from jax.sharding import PartitionSpec as P

D = 12288
BLOCK = 64
KEEP = 48
M = 4
TOK = 64
ROWS = M * TOK
DP = 4
TENSOR = 16
WIDTH = D // TENSOR
QUARTER = D // DP
EPSILON = 1e-05
LANES = 128
VMEM_LIMIT = 56 * 1024 * 1024


def build_kernel(rows_ref, blocks_ref, dense_ref):
    pair = pl.program_id(0)

    @pl.loop(0, D // 256)
    def _(chunk):
        dense_ref[pl.ds(pl.multiple_of(chunk * 256, 256), 256), :] = jnp.zeros((256, LANES), jnp.bfloat16)

    @pl.loop(0, KEEP)
    def _(kept):
        for half in range(2):
            first = pl.multiple_of(rows_ref[2 * pair + half, kept] * BLOCK, BLOCK)
            dense_ref[pl.ds(first, BLOCK), half * BLOCK:(half + 1) * BLOCK] = blocks_ref[half, kept]


def build_dense(values, rows_index):
    col_blocks = values.shape[0]
    blocks = values.reshape(col_blocks, KEEP, BLOCK, BLOCK)
    return pl.pallas_call(
        build_kernel,
        grid_spec=pltpu.PrefetchScalarGridSpec(
            num_scalar_prefetch=1,
            grid=(col_blocks // 2,),
            in_specs=[pl.BlockSpec((2, KEEP, BLOCK, BLOCK), lambda pair, rows: (pair, 0, 0, 0))],
            out_specs=pl.BlockSpec((D, LANES), lambda pair, rows: (0, pair)),
        ),
        out_shape=jax.ShapeDtypeStruct((D, col_blocks * BLOCK), jnp.bfloat16),
        compiler_params=pltpu.CompilerParams(vmem_limit_bytes=VMEM_LIMIT),
        cost_estimate=pl.CostEstimate(flops=0, bytes_accessed=32 * 1024 * 1024, transcendentals=0),
        name="build_dense",
    )(rows_index, blocks)


def layer_kernel(gathered_ref, weight_ref, gains_ref, own_ref, out_ref, stats_ref, rows, weight, total, row_sems, weight_sems):
    def row_copy(block):
        return pltpu.make_async_copy(gathered_ref.at[block], rows.at[block], row_sems.at[block])

    def weight_copy(block):
        span = pl.ds(pl.multiple_of(block * WIDTH, WIDTH), WIDTH)
        return pltpu.make_async_copy(weight_ref.at[span], weight.at[span], weight_sems.at[block])

    @pl.loop(0, TENSOR)
    def _(block):
        row_copy(block).start()

    @pl.loop(0, TENSOR)
    def _(block):
        weight_copy(block).start()

    def sums(block, carry):
        row_copy(block).wait()
        totals, squares = carry
        for part in range(WIDTH // LANES):
            values = rows[block, :, part * LANES:(part + 1) * LANES].astype(jnp.float32)
            totals = totals + values
            squares = squares + values * values
        return totals, squares

    zero = jnp.zeros((ROWS, LANES), jnp.float32)
    totals, squares = lax.fori_loop(0, TENSOR, sums, (zero, zero))
    mean = jnp.sum(totals, axis=1, keepdims=True) / D
    square = jnp.sum(squares, axis=1, keepdims=True) / D
    scale = lax.rsqrt(square - mean * mean + EPSILON)
    lane = lax.broadcasted_iota(jnp.int32, (ROWS, LANES), 1)
    stats_ref[...] = jnp.where(lane == 0, mean, scale)
    total[...] = own_ref[...].astype(jnp.float32)

    @pl.loop(0, TENSOR)
    def _(block):
        centre = stats_ref[:, 0:1]
        factor = stats_ref[:, 1:2]
        values = rows[block].astype(jnp.float32)
        normed = ((values - centre) * factor * gains_ref[pl.ds(block, 1), :]).astype(jnp.bfloat16)
        weight_copy(block).wait()
        span = pl.ds(pl.multiple_of(block * WIDTH, WIDTH), WIDTH)
        total[...] += jnp.dot(normed, weight[span], preferred_element_type=jnp.float32)

    out_ref[...] = total[...].astype(jnp.bfloat16)


def layer(gathered, weight, gains, own):
    vmem = pl.BlockSpec(memory_space=pltpu.VMEM)
    return pl.pallas_call(
        layer_kernel,
        in_specs=[pl.BlockSpec(memory_space=pl.ANY), pl.BlockSpec(memory_space=pl.ANY), vmem, vmem],
        out_specs=[vmem, vmem],
        out_shape=[
            jax.ShapeDtypeStruct((ROWS, WIDTH), jnp.bfloat16),
            jax.ShapeDtypeStruct((ROWS, LANES), jnp.float32),
        ],
        scratch_shapes=[
            pltpu.VMEM((TENSOR, ROWS, WIDTH), jnp.bfloat16),
            pltpu.VMEM((D, WIDTH), jnp.bfloat16),
            pltpu.VMEM((ROWS, WIDTH), jnp.float32),
            pltpu.SemaphoreType.DMA((TENSOR,)),
            pltpu.SemaphoreType.DMA((TENSOR,)),
        ],
        compiler_params=pltpu.CompilerParams(vmem_limit_bytes=VMEM_LIMIT),
        cost_estimate=pl.CostEstimate(flops=2 * ROWS * D * WIDTH, bytes_accessed=2 * D * (WIDTH + ROWS), transcendentals=ROWS),
        name="layer",
    )(gathered, weight, gains, own)


PIECE = 256


def gram_kernel(order_ref, rows_ref, *refs):
    cols_refs, stats_refs = refs[:DP], refs[DP:2 * DP]
    row_gain_ref, col_gain_ref, out_ref, cols = refs[2 * DP:]

    @pl.when((pl.program_id(0) == 0) & (pl.program_id(1) == 0))
    def _():
        for part in range(DP):
            values = cols_refs[part][...].astype(jnp.float32)
            scaled = (values - stats_refs[part][:, 0:1]) * stats_refs[part][:, 1:2]
            cols[part * ROWS:(part + 1) * ROWS, :] = (scaled * col_gain_ref[...]).astype(jnp.bfloat16)

    pieces = []
    for part in range(DP):
        values = rows_ref[order_ref[part], 0].astype(jnp.float32)
        scaled = (values - stats_refs[part][:, 0:1]) * stats_refs[part][:, 1:2]
        pieces.append((scaled * row_gain_ref[0]).astype(jnp.bfloat16))
    left = jnp.concatenate(pieces, axis=0)
    gram = lax.dot_general(left, cols[...], (((0,), (0,)), ((), ())), preferred_element_type=jnp.float32)
    out_ref[...] = gram * (2.0 / (DP * ROWS))


def gram(order, rows, cols, stats, row_gain, col_gain):
    per_block = WIDTH // PIECE
    whole = pl.BlockSpec((1, WIDTH), lambda block, piece, order: (0, 0))
    return pl.pallas_call(
        gram_kernel,
        grid_spec=pltpu.PrefetchScalarGridSpec(
            num_scalar_prefetch=1,
            grid=(DP, per_block),
            in_specs=[pl.BlockSpec((DP, 1, ROWS, PIECE), lambda block, piece, order: (0, block, 0, piece))]
            + [pl.BlockSpec((ROWS, WIDTH), lambda block, piece, order: (0, 0))] * DP
            + [pl.BlockSpec((ROWS, LANES), lambda block, piece, order: (0, 0))] * DP
            + [pl.BlockSpec((1, 1, PIECE), lambda block, piece, order: (block, 0, piece)), whole],
            out_specs=pl.BlockSpec((PIECE, WIDTH), lambda block, piece, order: (block * per_block + piece, 0)),
            scratch_shapes=[pltpu.VMEM((DP * ROWS, WIDTH), jnp.bfloat16)],
        ),
        out_shape=jax.ShapeDtypeStruct((QUARTER, WIDTH), jnp.float32),
        compiler_params=pltpu.CompilerParams(vmem_limit_bytes=VMEM_LIMIT),
        cost_estimate=pl.CostEstimate(
            flops=2 * DP * ROWS * QUARTER * WIDTH, bytes_accessed=4 * QUARTER * WIDTH + 2 * DP * ROWS * (QUARTER + WIDTH), transcendentals=0
        ),
        name="gram",
    )(order, rows, *cols, *stats, row_gain, col_gain)


def turn(value):
    pairs = [
        (d * TENSOR + q * DP + j, q * TENSOR + d * DP + j) for d in range(DP) for q in range(DP) for j in range(TENSOR // DP)
    ]
    return lax.ppermute(value, ("dp", "tensor"), pairs)


def gather_dp(value):
    return [value] + [
        lax.ppermute(value, "dp", [(source, (source + step) % DP) for source in range(DP)]) for step in range(1, DP)
    ]


def body(activations, gains, block_values, block_rows):
    first = lax.axis_index("pipe") == 0
    quarter = lax.axis_index("dp")
    gain = gains[0]
    own = activations.reshape(ROWS, WIDTH)
    with jax.named_scope("rows_first"):
        gathered = lax.all_gather(own, "tensor", axis=0)
    with jax.named_scope("gains"):
        all_gains = lax.all_to_all(jnp.broadcast_to(gain[None, :], (TENSOR, WIDTH)), "tensor", 0, 0, tiled=True)
    with jax.named_scope("weight"):
        weight = build_dense(block_values[0], block_rows[0])
    with jax.named_scope("layer_first"):
        updated_first, stats_first = layer(gathered, weight, all_gains, own)
    with jax.named_scope("hand_over"):
        received = lax.ppermute(updated_first, "pipe", [(0, 1)])
    with jax.named_scope("rows_second"):
        gathered = lax.all_gather(received, "tensor", axis=0)
    with jax.named_scope("hessian_inputs"):
        stream = jnp.where(first, own, received)
        turned = turn(stream)
        hessian_rows = lax.all_gather(turned, "tensor", axis=0)
        cols = gather_dp(stream)
    with jax.named_scope("layer_second"):
        updated_second, stats_second = layer(gathered, weight, all_gains, received)
    with jax.named_scope("hessian"):
        stats = gather_dp(jnp.where(first, stats_first, stats_second))
        row_gain = lax.dynamic_slice_in_dim(all_gains, quarter * (TENSOR // DP), TENSOR // DP, 0)
        order = (quarter - jnp.arange(DP, dtype=jnp.int32)) % DP
        hessian = gram(
            order, hessian_rows.reshape(DP, TENSOR // DP, ROWS, WIDTH), cols, stats, row_gain[:, None, :], gain[None, :]
        )
    sections = jnp.where(first, updated_first, updated_second)
    return (hessian[None], sections.reshape(1, M, TOK, WIDTH))


def solution(mesh):
    return jax.shard_map(
        body,
        mesh=mesh,
        in_specs=(
            P(None, "dp", "tensor"),
            P("pipe", "tensor"),
            P("pipe", "tensor", None, None),
            P("pipe", "tensor", None),
        ),
        out_specs=(P("pipe", "dp", "tensor"), P("pipe", None, "dp", "tensor")),
        check_vma=False,
    )
```

```python
import jax
import jax.numpy as jnp
from jax import lax
from jax.experimental import pallas as pl
from jax.experimental.pallas import tpu as pltpu
from jax.sharding import PartitionSpec as P

D = 12288
BLOCK = 64
KEEP = 48
M = 4
TOK = 64
ROWS = M * TOK
DP = 4
TENSOR = 16
WIDTH = D // TENSOR
QUARTER = D // DP
EPSILON = 1e-05
LANES = 128
SPAN = 256
CHUNK = 64
MIB = 1024 * 1024
VMEM_LIMIT = 61 * MIB
NEAR = [(dz, dy) for dz in range(2) for dy in range(4)]
ANY = pl.BlockSpec(memory_space=pl.ANY)
VMEM = pl.BlockSpec(memory_space=pltpu.VMEM)
SMEM = pl.BlockSpec(memory_space=pltpu.SMEM)


def build_kernel(rows_ref, blocks_ref, dense_ref):
    group = pl.program_id(0)

    @pl.loop(0, D // SPAN)
    def _(chunk):
        dense_ref[0, pl.ds(pl.multiple_of(chunk * SPAN, SPAN), SPAN), :] = jnp.zeros((SPAN, SPAN), jnp.bfloat16)

    per = SPAN // BLOCK

    @pl.loop(0, KEEP, unroll=4)
    def _(kept):
        for part in range(per):
            first = pl.multiple_of(rows_ref[per * group + part, kept] * BLOCK, BLOCK)
            dense_ref[0, pl.ds(first, BLOCK), part * BLOCK:(part + 1) * BLOCK] = blocks_ref[part, kept]


def build_dense(values, rows_index):
    blocks = values.reshape(WIDTH // BLOCK, KEEP, BLOCK, BLOCK)
    per = SPAN // BLOCK
    return pl.pallas_call(
        build_kernel,
        grid_spec=pltpu.PrefetchScalarGridSpec(
            num_scalar_prefetch=1,
            grid=(WIDTH // SPAN,),
            in_specs=[pl.BlockSpec((per, KEEP, BLOCK, BLOCK), lambda group, rows: (group, 0, 0, 0))],
            out_specs=pl.BlockSpec((1, D, SPAN), lambda group, rows: (group, 0, 0)),
        ),
        out_shape=jax.ShapeDtypeStruct((WIDTH // SPAN, D, SPAN), jnp.bfloat16),
        compiler_params=pltpu.CompilerParams(vmem_limit_bytes=VMEM_LIMIT),
        cost_estimate=pl.CostEstimate(flops=0, bytes_accessed=32 * MIB, transcendentals=0),
        name="build_dense",
    )(rows_index, blocks)


def start_pieces(pieces, refs, rows, sems):
    for array, start, count, position, into in pieces:
        pltpu.make_async_copy(
            refs[array].at[pl.ds(start, count)], rows.at[position, pl.ds(into, count)], sems.at[position]
        ).start()


def wait_block(rows, sems, position):
    pltpu.make_async_copy(rows.at[position], rows.at[position], sems.at[position]).wait()


def spread(column, means, span):
    means[span] = jnp.broadcast_to(column, (ROWS, LANES))


def block_at(spot_ref, position):
    side, (dz, dy) = position // len(NEAR), NEAR[position % len(NEAR)]
    z, y, core = (lax.rem(spot_ref[1 + axis] + step, size) for axis, (step, size) in enumerate([(dz, 2), (dy, 4), (side, 2)]))
    return z * 8 + y * 2 + core


def layer_kernel(pieces, count, straight, spot_ref, weight_ref, gains_ref, own_ref, *refs):
    sources, (out_ref, stats_ref, rows, weight, total, means, scales, sems, weight_sems) = refs[:count], refs[count:]

    def place(position):
        return position if straight else block_at(spot_ref, position)

    def weight_copy(position):
        span = pl.ds(pl.multiple_of(place(position) * WIDTH, WIDTH), WIDTH)
        into = pl.ds(position * WIDTH, WIDTH)
        return pltpu.make_async_copy(weight_ref.at[:, span], weight.at[:, into], weight_sems.at[position])

    start_pieces(pieces, sources, rows, sems)
    means[...] = jnp.zeros_like(means)
    scales[...] = jnp.zeros_like(scales)
    total[...] = own_ref[...].astype(jnp.float32)
    for position in range(TENSOR):
        wait_block(rows, sems, position)
        for chunk in range(0, ROWS, CHUNK):
            span = slice(chunk, chunk + CHUNK)
            added = jnp.zeros((CHUNK, LANES), jnp.float32)
            squared = added
            for part in range(WIDTH // LANES):
                values = rows[position, span, part * LANES:(part + 1) * LANES].astype(jnp.float32)
                added = added + values
                squared = squared + values * values
            means[span] += added
            scales[span] += squared
        if position % 2:
            weight_copy(position // 2).start()
    mean = jnp.sum(means[...], axis=1, keepdims=True) / D
    square = jnp.sum(scales[...], axis=1, keepdims=True) / D
    scale = lax.rsqrt(square - mean * mean + EPSILON)
    lane = lax.broadcasted_iota(jnp.int32, (ROWS, LANES), 1)
    stats_ref[...] = jnp.where(lane == 0, mean, scale)
    spread(mean, means, slice(0, ROWS))
    spread(scale, scales, slice(0, ROWS))

    def normalise(position):
        gain = gains_ref[place(position)]
        for chunk in range(0, ROWS, CHUNK):
            span = slice(chunk, chunk + CHUNK)
            for part in range(WIDTH // LANES):
                lanes = slice(part * LANES, (part + 1) * LANES)
                values = rows[position, span, lanes].astype(jnp.float32)
                scaled = (values - means[span]) * scales[span] * gain[:, lanes]
                rows[position, span, lanes] = scaled.astype(jnp.bfloat16)

    normalise(0)
    normalise(1)
    for position in range(0, TENSOR, 2):
        left = jnp.concatenate([rows[position], rows[position + 1]], axis=1)
        for later in range(position + TENSOR // 2, min(position + TENSOR // 2 + 2, TENSOR)):
            weight_copy(later).start()
        weight_copy(position).wait()
        weight_copy(position + 1).wait()
        for group in range(WIDTH // SPAN):
            lanes = slice(group * SPAN, (group + 1) * SPAN)
            right = weight[group, position * WIDTH:(position + 2) * WIDTH]
            total[:, lanes] += jnp.dot(left, right, preferred_element_type=jnp.float32)
        if position + 2 < TENSOR:
            normalise(position + 2)
            normalise(position + 3)
    out_ref[...] = total[...].astype(jnp.bfloat16)


def in_hbm(arrays):
    return [pltpu.with_memory_space_constraint(array, pltpu.HBM) for array in arrays]


def layer(spot, gathered, pieces, weight, gains, own, straight):
    count = len(gathered)
    return pl.pallas_call(
        lambda *refs: layer_kernel(pieces, count, straight, *refs),
        in_specs=[SMEM, ANY, VMEM, VMEM] + [ANY] * count,
        out_specs=[VMEM, VMEM],
        out_shape=[
            jax.ShapeDtypeStruct((ROWS, WIDTH), jnp.bfloat16),
            jax.ShapeDtypeStruct((ROWS, LANES), jnp.float32),
        ],
        scratch_shapes=[
            pltpu.VMEM((TENSOR, ROWS, WIDTH), jnp.bfloat16),
            pltpu.VMEM((WIDTH // SPAN, D, SPAN), jnp.bfloat16),
            pltpu.VMEM((ROWS, WIDTH), jnp.float32),
            pltpu.VMEM((ROWS, LANES), jnp.float32),
            pltpu.VMEM((ROWS, LANES), jnp.float32),
            pltpu.SemaphoreType.DMA((TENSOR,)),
            pltpu.SemaphoreType.DMA((TENSOR,)),
        ],
        compiler_params=pltpu.CompilerParams(vmem_limit_bytes=VMEM_LIMIT),
        cost_estimate=pl.CostEstimate(flops=2 * ROWS * D * WIDTH, bytes_accessed=2 * D * (WIDTH + ROWS), transcendentals=ROWS),
        name="layer",
    )(spot, *in_hbm([weight]), gains, own, *in_hbm(gathered))


PIECE = 384
PER = WIDTH // PIECE
STEPS = QUARTER // PIECE
HALF = TENSOR // DP // 2
CLASSES = [(side, half) for side in range(2) for half in range(HALF)]


def pick_kernel(pieces, count, spot_ref, *refs):
    sources, picked, sems = refs[:count], refs[count:-1], refs[-1]
    for step in range(DP):
        target = lax.rem(spot_ref[0] + step, DP)
        for half in range(HALF):
            dz = lax.rem(target // 2 + 2 - spot_ref[1], 2)
            dy = lax.rem(lax.rem(target, 2) * 2 + half + 4 - spot_ref[2], 4)
            for position in range(len(NEAR)):

                @pl.when(dz * 4 + dy == position)
                def _():
                    for array, start, size, at, row in pieces:
                        if at == position:
                            pltpu.make_async_copy(
                                sources[array].at[pl.ds(start, size)],
                                picked[step].at[pl.ds(half * ROWS + row, size)],
                                sems.at[step, half],
                            ).start()

    for step in range(DP):
        for half in range(HALF):
            block = picked[step].at[pl.ds(half * ROWS, ROWS)]
            pltpu.make_async_copy(block, block, sems.at[step, half]).wait()


def pick(spot, gathered, pieces):
    count = len(gathered)
    return pl.pallas_call(
        lambda *refs: pick_kernel(pieces, count, *refs),
        in_specs=[SMEM] + [ANY] * count,
        out_specs=[VMEM] * DP,
        out_shape=[jax.ShapeDtypeStruct((HALF * ROWS, WIDTH), jnp.bfloat16)] * DP,
        scratch_shapes=[pltpu.SemaphoreType.DMA((DP, HALF))],
        compiler_params=pltpu.CompilerParams(vmem_limit_bytes=VMEM_LIMIT),
        cost_estimate=pl.CostEstimate(flops=0, bytes_accessed=4 * DP * HALF * ROWS * WIDTH, transcendentals=0),
        name="pick",
    )(spot, *in_hbm(gathered))


def after(values, others):
    count = len(values)
    return pl.pallas_call(
        lambda *refs: None,
        in_specs=[ANY] * (count + len(others)),
        out_specs=[ANY] * count,
        out_shape=[jax.ShapeDtypeStruct(value.shape, value.dtype) for value in values],
        input_output_aliases={place: place for place in range(count)},
        name="after",
    )(*in_hbm(values), *others)


def gram_kernel(spot_ref, *refs):
    sources, stats_refs, refs = refs[:2 * DP], refs[2 * DP:3 * DP], refs[3 * DP:]
    cols_ref, row_gain_ref, col_gain_ref, out_ref, rows, cols, means, scales, left, result, sems, row_sems = refs

    def block_of(group):
        side, half = CLASSES[group]
        return lax.rem(spot_ref[3] + side, 2) + 2 * half

    def row_copies(group):
        side, half = CLASSES[group]
        return [
            pltpu.make_async_copy(
                sources[side * DP + part].at[pl.ds(half * ROWS, ROWS)], rows.at[group, part], row_sems.at[group, part]
            )
            for part in range(DP)
        ]

    for group in range(len(CLASSES)):
        for copy in row_copies(group):
            copy.start()
    for part in range(DP):
        spread(stats_refs[part][:, 0:1], means, slice(part * ROWS, (part + 1) * ROWS))
        spread(stats_refs[part][:, 1:2], scales, slice(part * ROWS, (part + 1) * ROWS))
        for chunk in range(0, ROWS, CHUNK):
            span = slice(part * ROWS + chunk, part * ROWS + chunk + CHUNK)
            for lane in range(WIDTH // LANES):
                lanes = slice(lane * LANES, (lane + 1) * LANES)
                values = cols_ref[lax.rem(spot_ref[0] + DP - part, DP), chunk:chunk + CHUNK, lanes].astype(jnp.float32)
                scaled = (values - means[span]) * scales[span] * col_gain_ref[:, lanes]
                cols[span, lanes] = scaled.astype(jnp.bfloat16)

    def normalise(step):
        group, base = step // PER, step % PER * PIECE
        if base == 0:
            for copy in row_copies(group):
                copy.wait()
        gain = row_gain_ref[block_of(group)]
        for part in range(DP):
            for chunk in range(0, ROWS, CHUNK):
                span = slice(part * ROWS + chunk, part * ROWS + chunk + CHUNK)
                for lane in range(PIECE // LANES):
                    from_lanes = slice(base + lane * LANES, base + (lane + 1) * LANES)
                    values = rows[group, part, chunk:chunk + CHUNK, from_lanes].astype(jnp.float32)
                    scaled = (values - means[span]) * scales[span] * gain[:, from_lanes]
                    left[step % 2, span, lane * LANES:(lane + 1) * LANES] = scaled.astype(jnp.bfloat16)

    def store(step):
        row = pl.multiple_of(block_of(step // PER) * WIDTH + step % PER * PIECE, PIECE)
        return pltpu.make_async_copy(result.at[step % 2], out_ref.at[pl.ds(row, PIECE)], sems.at[step % 2])

    normalise(0)
    for step in range(STEPS):
        product = lax.dot_general(
            left[step % 2], cols[...], (((0,), (0,)), ((), ())), preferred_element_type=jnp.float32
        )
        if step >= 2:
            store(step - 2).wait()
        result[step % 2] = product * (2.0 / (DP * ROWS))
        store(step).start()
        if step + 1 < STEPS:
            normalise(step + 1)
    store(STEPS - 2).wait()
    store(STEPS - 1).wait()


def gram(spot, rows, cols, stats, row_gain, col_gain):
    return pl.pallas_call(
        gram_kernel,
        in_specs=[SMEM] + [ANY] * (2 * DP) + [VMEM] * (DP + 3),
        out_specs=ANY,
        out_shape=jax.ShapeDtypeStruct((QUARTER, WIDTH), jnp.float32),
        scratch_shapes=[
            pltpu.VMEM((len(CLASSES), DP, ROWS, WIDTH), jnp.bfloat16),
            pltpu.VMEM((DP * ROWS, WIDTH), jnp.bfloat16),
            pltpu.VMEM((DP * ROWS, LANES), jnp.float32),
            pltpu.VMEM((DP * ROWS, LANES), jnp.float32),
            pltpu.VMEM((2, DP * ROWS, PIECE), jnp.bfloat16),
            pltpu.VMEM((2, PIECE, WIDTH), jnp.float32),
            pltpu.SemaphoreType.DMA((2,)),
            pltpu.SemaphoreType.DMA((len(CLASSES), DP)),
        ],
        compiler_params=pltpu.CompilerParams(vmem_limit_bytes=VMEM_LIMIT),
        cost_estimate=pl.CostEstimate(
            flops=2 * DP * ROWS * QUARTER * WIDTH, bytes_accessed=4 * QUARTER * WIDTH + 2 * DP * ROWS * (QUARTER + WIDTH), transcendentals=0
        ),
        name="gram",
    )(spot, *rows, *stats, cols, row_gain, col_gain)


def along_dp(value, step):
    return lax.ppermute(value, "dp", [(source, (source + step) % DP) for source in range(DP)])


def gather_dp(value):
    return [value] + [along_dp(value, step) for step in range(1, DP)]


def tensor_at(z, y, core):
    return (z % 2) * 8 + (y % 4) * 2 + core % 2


def shift(value, z, y, core):
    pairs = [
        (tensor_at(a, b, c), tensor_at(a + z, b + y, c + core)) for a in range(2) for b in range(4) for c in range(2)
    ]
    return lax.ppermute(value, "tensor", pairs)


def gather_near(value):
    rows = value.shape[0]
    cut, cut2 = rows * 3 // 8, rows * 11 // 16
    up, down, over = shift(value, 0, 1, 0), shift(value, 0, -1, 0), shift(value, 1, 0, 0)
    up2, over_up, over_down = shift(up, 0, 1, 0), shift(up, 1, 0, 0), shift(over, 0, -1, 0)
    far = [
        shift(up2[:cut], 1, 0, 0),
        shift(over_up[cut:cut2], 0, 1, 0),
        shift(over_down[cut2:], 0, -1, 0),
    ]
    mine = [value, down, up2, up, over, over_down, over_up] + far
    theirs = [shift(array, 0, 0, 1) for array in mine]
    pieces = []
    for side in range(2):
        at, pos = side * len(mine), side * len(NEAR)
        pieces += [(at + array, 0, rows, pos + position, 0) for array, position in enumerate([0, 1, 2, 3, 4, 5, 7])]
        pieces += [
            (at + 7, 0, cut, pos + 6, 0),
            (at + 8, 0, cut2 - cut, pos + 6, cut),
            (at + 9, 0, rows - cut2, pos + 6, cut2),
        ]
    return mine + theirs, pieces


def body(activations, gains, block_values, block_rows):
    first = lax.axis_index("pipe") == 0
    quarter = lax.axis_index("dp")
    here = lax.axis_index("tensor")
    gain = gains[0]
    own = activations.reshape(ROWS, WIDTH)
    with jax.named_scope("rows_first"):
        gathered = lax.all_gather(own, "tensor", axis=0, tiled=True)
    with jax.named_scope("gains"):
        all_gains = lax.all_to_all(jnp.broadcast_to(gain[None, :], (TENSOR, WIDTH)), "tensor", 0, 0, tiled=True)
        all_gains = all_gains[:, None, :]
    with jax.named_scope("weight"):
        weight = build_dense(block_values[0], block_rows[0])
    spot = jnp.stack([quarter, here // 8, here // 2 % 4, here % 2]).astype(jnp.int32)
    with jax.named_scope("layer_first"):
        pieces = [(0, block * ROWS, ROWS, block, 0) for block in range(TENSOR)]
        updated_first, _ = layer(spot, [gathered], pieces, weight, all_gains, own, True)
    with jax.named_scope("hand_over"):
        received = lax.ppermute(updated_first, "pipe", [(0, 1)])
    stream = jnp.where(first, own, received)
    with jax.named_scope("columns"):
        cols = lax.all_gather(jnp.where(first, own, 0) + received, "dp", axis=0)
    with jax.named_scope("rows_second"):
        arrays, pieces = gather_near(stream)
    with jax.named_scope("hessian_rows"):
        mine = len(arrays) // 2
        picked = pick(spot, arrays[:mine], [piece for piece in pieces if piece[0] < mine])
        rows = [along_dp(picked[step], step) for step in range(1, DP)]
    with jax.named_scope("layer_second"):
        updated_second, stats = layer(spot, arrays, pieces, weight, all_gains, stream, False)
        stats = gather_dp(stats)
    with jax.named_scope("hessian"):
        near = after([rows[0], rows[2]], [stats[0]])
        far = after([rows[1]], [near[0]] + stats[1:])
        rows = [picked[0], near[0], far[0], near[1]]
        rows += [shift(value, 0, 0, 1) for value in rows]
        row_gain = lax.dynamic_slice_in_dim(all_gains, quarter * (TENSOR // DP), TENSOR // DP, 0)
        hessian = gram(spot, rows, cols, stats, row_gain, gain[None, :])
    sections = jnp.where(first, updated_first, updated_second)
    return (hessian[None], sections.reshape(1, M, TOK, WIDTH))


def solution(mesh):
    return jax.shard_map(
        body,
        mesh=mesh,
        in_specs=(
            P(None, "dp", "tensor"),
            P("pipe", "tensor"),
            P("pipe", "tensor", None, None),
            P("pipe", "tensor", None),
        ),
        out_specs=(P("pipe", "dp", "tensor"), P("pipe", None, "dp", "tensor")),
        check_vma=False,
    )
```

```python
import jax
import jax.numpy as jnp
from jax import lax
from jax.experimental import pallas as pl
from jax.experimental.pallas import tpu as pltpu
from jax.sharding import PartitionSpec as P

D = 12288
BLOCK = 64
KEEP = 48
M = 4
TOK = 64
ROWS = M * TOK
DP = 4
TENSOR = 16
WIDTH = D // TENSOR
QUARTER = D // DP
EPSILON = 1e-05
LANES = 128
SPAN = 256
CHUNK = 64
MIB = 1024 * 1024
VMEM_LIMIT = 61 * MIB
NEAR = [(dz, dy) for dz in range(2) for dy in range(4)]
ANY = pl.BlockSpec(memory_space=pl.ANY)
VMEM = pl.BlockSpec(memory_space=pltpu.VMEM)
SMEM = pl.BlockSpec(memory_space=pltpu.SMEM)


def build_kernel(rows_ref, blocks_ref, dense_ref):
    group = pl.program_id(0)

    @pl.loop(0, D // SPAN)
    def _(chunk):
        dense_ref[0, pl.ds(pl.multiple_of(chunk * SPAN, SPAN), SPAN), :] = jnp.zeros((SPAN, SPAN), jnp.bfloat16)

    per = SPAN // BLOCK

    @pl.loop(0, KEEP, unroll=4)
    def _(kept):
        for part in range(per):
            first = pl.multiple_of(rows_ref[per * group + part, kept] * BLOCK, BLOCK)
            dense_ref[0, pl.ds(first, BLOCK), part * BLOCK:(part + 1) * BLOCK] = blocks_ref[part, kept]


def build_dense(values, rows_index):
    blocks = values.reshape(WIDTH // BLOCK, KEEP, BLOCK, BLOCK)
    per = SPAN // BLOCK
    return pl.pallas_call(
        build_kernel,
        grid_spec=pltpu.PrefetchScalarGridSpec(
            num_scalar_prefetch=1,
            grid=(WIDTH // SPAN,),
            in_specs=[pl.BlockSpec((per, KEEP, BLOCK, BLOCK), lambda group, rows: (group, 0, 0, 0))],
            out_specs=pl.BlockSpec((1, D, SPAN), lambda group, rows: (group, 0, 0)),
        ),
        out_shape=jax.ShapeDtypeStruct((WIDTH // SPAN, D, SPAN), jnp.bfloat16),
        compiler_params=pltpu.CompilerParams(vmem_limit_bytes=VMEM_LIMIT),
        cost_estimate=pl.CostEstimate(flops=0, bytes_accessed=32 * MIB, transcendentals=0),
        name="build_dense",
    )(rows_index, blocks)


def start_pieces(pieces, refs, rows, sems):
    for array, start, count, position, into in pieces:
        pltpu.make_async_copy(
            refs[array].at[pl.ds(start, count)], rows.at[position, pl.ds(into, count)], sems.at[position]
        ).start()


def wait_block(rows, sems, position):
    pltpu.make_async_copy(rows.at[position], rows.at[position], sems.at[position]).wait()


def spread(column, means, span):
    means[span] = jnp.broadcast_to(column, (ROWS, LANES))


def block_at(spot_ref, position):
    side, (dz, dy) = position // len(NEAR), NEAR[position % len(NEAR)]
    z, y, core = (lax.rem(spot_ref[1 + axis] + step, size) for axis, (step, size) in enumerate([(dz, 2), (dy, 4), (side, 2)]))
    return z * 8 + y * 2 + core


def layer_kernel(pieces, count, straight, spot_ref, weight_ref, gains_ref, own_ref, *refs):
    sources, (out_ref, stats_ref, rows, weight, total, means, scales, sems, weight_sems) = refs[:count], refs[count:]

    def place(position):
        return position if straight else block_at(spot_ref, position)

    def weight_copy(position):
        span = pl.ds(pl.multiple_of(place(position) * WIDTH, WIDTH), WIDTH)
        into = pl.ds(position * WIDTH, WIDTH)
        return pltpu.make_async_copy(weight_ref.at[:, span], weight.at[:, into], weight_sems.at[position])

    start_pieces(pieces, sources, rows, sems)
    means[...] = jnp.zeros_like(means)
    scales[...] = jnp.zeros_like(scales)
    total[...] = own_ref[...].astype(jnp.float32)
    for position in range(TENSOR):
        wait_block(rows, sems, position)
        for chunk in range(0, ROWS, CHUNK):
            span = slice(chunk, chunk + CHUNK)
            added = jnp.zeros((CHUNK, LANES), jnp.float32)
            squared = added
            for part in range(WIDTH // LANES):
                values = rows[position, span, part * LANES:(part + 1) * LANES].astype(jnp.float32)
                added = added + values
                squared = squared + values * values
            means[span] += added
            scales[span] += squared
        if position % 2:
            weight_copy(position // 2).start()
    mean = jnp.sum(means[...], axis=1, keepdims=True) / D
    square = jnp.sum(scales[...], axis=1, keepdims=True) / D
    scale = lax.rsqrt(square - mean * mean + EPSILON)
    lane = lax.broadcasted_iota(jnp.int32, (ROWS, LANES), 1)
    stats_ref[...] = jnp.transpose(jnp.where(lane == 0, mean, scale))[:8]
    spread(mean, means, slice(0, ROWS))
    spread(scale, scales, slice(0, ROWS))

    def normalise(position):
        gain = gains_ref[place(position)]
        for chunk in range(0, ROWS, CHUNK):
            span = slice(chunk, chunk + CHUNK)
            for part in range(WIDTH // LANES):
                lanes = slice(part * LANES, (part + 1) * LANES)
                values = rows[position, span, lanes].astype(jnp.float32)
                scaled = (values - means[span]) * scales[span] * gain[:, lanes]
                rows[position, span, lanes] = scaled.astype(jnp.bfloat16)

    normalise(0)
    normalise(1)
    for position in range(0, TENSOR, 2):
        left = jnp.concatenate([rows[position], rows[position + 1]], axis=1)
        for later in range(position + TENSOR // 2, min(position + TENSOR // 2 + 2, TENSOR)):
            weight_copy(later).start()
        weight_copy(position).wait()
        weight_copy(position + 1).wait()
        for group in range(WIDTH // SPAN):
            lanes = slice(group * SPAN, (group + 1) * SPAN)
            right = weight[group, position * WIDTH:(position + 2) * WIDTH]
            total[:, lanes] += jnp.dot(left, right, preferred_element_type=jnp.float32)
        if position + 2 < TENSOR:
            normalise(position + 2)
            normalise(position + 3)
    out_ref[...] = total[...].astype(jnp.bfloat16)


def in_hbm(arrays):
    return [pltpu.with_memory_space_constraint(array, pltpu.HBM) for array in arrays]


def layer(spot, gathered, pieces, weight, gains, own, straight):
    count = len(gathered)
    return pl.pallas_call(
        lambda *refs: layer_kernel(pieces, count, straight, *refs),
        in_specs=[SMEM, ANY, VMEM, VMEM] + [ANY] * count,
        out_specs=[VMEM, VMEM],
        out_shape=[
            jax.ShapeDtypeStruct((ROWS, WIDTH), jnp.bfloat16),
            jax.ShapeDtypeStruct((8, ROWS), jnp.float32),
        ],
        scratch_shapes=[
            pltpu.VMEM((TENSOR, ROWS, WIDTH), jnp.bfloat16),
            pltpu.VMEM((WIDTH // SPAN, D, SPAN), jnp.bfloat16),
            pltpu.VMEM((ROWS, WIDTH), jnp.float32),
            pltpu.VMEM((ROWS, LANES), jnp.float32),
            pltpu.VMEM((ROWS, LANES), jnp.float32),
            pltpu.SemaphoreType.DMA((TENSOR,)),
            pltpu.SemaphoreType.DMA((TENSOR,)),
        ],
        compiler_params=pltpu.CompilerParams(vmem_limit_bytes=VMEM_LIMIT),
        cost_estimate=pl.CostEstimate(flops=2 * ROWS * D * WIDTH, bytes_accessed=2 * D * (WIDTH + ROWS), transcendentals=ROWS),
        name="layer",
    )(spot, *in_hbm([weight]), gains, own, *in_hbm(gathered))


PIECE = 384
PER = WIDTH // PIECE
STEPS = QUARTER // PIECE
HALF = TENSOR // DP // 2
CLASSES = [(side, half) for side in range(2) for half in range(HALF)]


def half_at(spot_ref, step):
    return spot_ref[1] if step == 2 else lax.rem(spot_ref[2], 2)


def pick_kernel(pieces, count, spot_ref, *refs):
    sources, picked, sems = refs[:count], refs[count + 1:-1], refs[-1]
    jobs = [(0, 0, 0), (0, 1, 1)] + [(step, half_at(spot_ref, step), 0) for step in range(1, DP)]
    for job, (step, half, into) in enumerate(jobs):
        target = lax.rem(spot_ref[0] + step, DP)
        dz = lax.rem(target // 2 + 2 - spot_ref[1], 2)
        dy = lax.rem(lax.rem(target, 2) * 2 + half + 4 - spot_ref[2], 4)
        for position in range(len(NEAR)):

            @pl.when(dz * 4 + dy == position)
            def _():
                for array, start, size, at, row in pieces:
                    if at == position:
                        pltpu.make_async_copy(
                            sources[array].at[pl.ds(start, size)],
                            picked[step].at[pl.ds(into * ROWS + row, size)],
                            sems.at[job],
                        ).start()

    for job, (step, _, into) in enumerate(jobs):
        block = picked[step].at[pl.ds(into * ROWS, ROWS)]
        pltpu.make_async_copy(block, block, sems.at[job]).wait()


def pick(spot, gathered, pieces, before):
    count = len(gathered)
    return pl.pallas_call(
        lambda *refs: pick_kernel(pieces, count, *refs),
        in_specs=[SMEM] + [ANY] * (count + 1),
        out_specs=[VMEM] * DP,
        out_shape=[jax.ShapeDtypeStruct((rows, WIDTH), jnp.bfloat16) for rows in [HALF * ROWS] + [ROWS] * (DP - 1)],
        scratch_shapes=[pltpu.SemaphoreType.DMA((DP + 1,))],
        compiler_params=pltpu.CompilerParams(vmem_limit_bytes=VMEM_LIMIT),
        cost_estimate=pl.CostEstimate(flops=0, bytes_accessed=4 * (DP + 1) * ROWS * WIDTH, transcendentals=0),
        name="pick",
    )(spot, *in_hbm(gathered), before)


def after(values, others):
    count = len(values)
    return pl.pallas_call(
        lambda *refs: None,
        in_specs=[ANY] * (count + len(others)),
        out_specs=[ANY] * count,
        out_shape=[jax.ShapeDtypeStruct(value.shape, value.dtype) for value in values],
        input_output_aliases={place: place for place in range(count)},
        name="after",
    )(*in_hbm(values), *others)


def gram_kernel(spot_ref, *refs):
    near, far, refs = refs[:2 * DP], refs[2 * DP:4 * DP - 2], refs[4 * DP - 2:]
    stats_refs, refs = refs[:DP], refs[DP:]
    cols_ref, gains_ref, col_gain_ref, out_ref, rows, cols, means, scales, left, result, sems, row_sems = refs

    def block_of(group):
        side, half = CLASSES[group]
        return lax.rem(spot_ref[3] + side, 2) + 2 * half

    def row_copy(source, group, part):
        return pltpu.make_async_copy(source, rows.at[group, part], row_sems.at[group, part])

    def start_rows(side):
        for half in range(HALF):
            row_copy(near[side * DP].at[pl.ds(half * ROWS, ROWS)], side * HALF + half, 0).start()
        for part in range(1, DP):
            half = half_at(spot_ref, part)
            row_copy(near[side * DP + part], side * HALF + half, part).start()
            row_copy(far[side * (DP - 1) + part - 1], side * HALF + 1 - half, part).start()

    start_rows(0)
    for part in range(DP):
        span = slice(part * ROWS, (part + 1) * ROWS)
        means[span] = jnp.transpose(jnp.broadcast_to(stats_refs[part][0:1], (LANES, ROWS)))
        scales[span] = jnp.transpose(jnp.broadcast_to(stats_refs[part][1:2], (LANES, ROWS)))
        for chunk in range(0, ROWS, CHUNK):
            span = slice(part * ROWS + chunk, part * ROWS + chunk + CHUNK)
            for lane in range(WIDTH // LANES):
                lanes = slice(lane * LANES, (lane + 1) * LANES)
                values = cols_ref[lax.rem(spot_ref[0] + DP - part, DP), chunk:chunk + CHUNK, lanes].astype(jnp.float32)
                scaled = (values - means[span]) * scales[span] * col_gain_ref[:, lanes]
                cols[span, lanes] = scaled.astype(jnp.bfloat16)

    def normalise(step):
        group, base = step // PER, step % PER * PIECE
        if base == 0:
            for part in range(DP):
                row_copy(rows.at[group, part], group, part).wait()
        gain = gains_ref[spot_ref[0] * (TENSOR // DP) + block_of(group)]
        for part in range(DP):
            for chunk in range(0, ROWS, CHUNK):
                span = slice(part * ROWS + chunk, part * ROWS + chunk + CHUNK)
                for lane in range(PIECE // LANES):
                    from_lanes = slice(base + lane * LANES, base + (lane + 1) * LANES)
                    values = rows[group, part, chunk:chunk + CHUNK, from_lanes].astype(jnp.float32)
                    scaled = (values - means[span]) * scales[span] * gain[:, from_lanes]
                    left[step % 2, span, lane * LANES:(lane + 1) * LANES] = scaled.astype(jnp.bfloat16)

    def store(step):
        row = pl.multiple_of(block_of(step // PER) * WIDTH + step % PER * PIECE, PIECE)
        return pltpu.make_async_copy(result.at[step % 2], out_ref.at[pl.ds(row, PIECE)], sems.at[step % 2])

    normalise(0)
    start_rows(1)
    for step in range(STEPS):
        product = lax.dot_general(
            left[step % 2], cols[...], (((0,), (0,)), ((), ())), preferred_element_type=jnp.float32
        )
        if step >= 2:
            store(step - 2).wait()
        result[step % 2] = product * (2.0 / (DP * ROWS))
        store(step).start()
        if step + 1 < STEPS:
            normalise(step + 1)
    store(STEPS - 2).wait()
    store(STEPS - 1).wait()


def gram(spot, near, far, cols, stats, gains, col_gain):
    return pl.pallas_call(
        gram_kernel,
        in_specs=[SMEM] + [ANY] * (4 * DP - 2) + [VMEM] * (DP + 3),
        out_specs=ANY,
        out_shape=jax.ShapeDtypeStruct((QUARTER, WIDTH), jnp.float32),
        scratch_shapes=[
            pltpu.VMEM((len(CLASSES), DP, ROWS, WIDTH), jnp.bfloat16),
            pltpu.VMEM((DP * ROWS, WIDTH), jnp.bfloat16),
            pltpu.VMEM((DP * ROWS, LANES), jnp.float32),
            pltpu.VMEM((DP * ROWS, LANES), jnp.float32),
            pltpu.VMEM((2, DP * ROWS, PIECE), jnp.bfloat16),
            pltpu.VMEM((2, PIECE, WIDTH), jnp.float32),
            pltpu.SemaphoreType.DMA((2,)),
            pltpu.SemaphoreType.DMA((len(CLASSES), DP)),
        ],
        compiler_params=pltpu.CompilerParams(vmem_limit_bytes=VMEM_LIMIT),
        cost_estimate=pl.CostEstimate(
            flops=2 * DP * ROWS * QUARTER * WIDTH, bytes_accessed=4 * QUARTER * WIDTH + 2 * DP * ROWS * (QUARTER + WIDTH), transcendentals=0
        ),
        name="gram",
    )(spot, *near, *far, *stats, cols, gains, col_gain)


def along_dp(value, step):
    return lax.ppermute(value, "dp", [(source, (source + step) % DP) for source in range(DP)])


def gather_dp(value):
    return [value] + [along_dp(value, step) for step in range(1, DP)]


def tensor_at(z, y, core):
    return (z % 2) * 8 + (y % 4) * 2 + core % 2


def shift(value, z, y, core):
    pairs = [
        (tensor_at(a, b, c), tensor_at(a + z, b + y, c + core)) for a in range(2) for b in range(4) for c in range(2)
    ]
    return lax.ppermute(value, "tensor", pairs)


def share(value, step):
    pairs = []
    for z in range(2):
        for y in range(4):
            for core in range(2):
                to = {1: (z, y ^ 1), 2: (1 - z, y), 3: (z, 3 - y)}[step]
                pairs.append((tensor_at(z, y, core), tensor_at(*to, core)))
    return lax.ppermute(value, "tensor", pairs)


def gather_near(value):
    rows = value.shape[0]
    cut, cut2 = rows * 3 // 8, rows * 11 // 16
    up, down, over = shift(value, 0, 1, 0), shift(value, 0, -1, 0), shift(value, 1, 0, 0)
    up2, over_up, over_down = shift(up, 0, 1, 0), shift(up, 1, 0, 0), shift(over, 0, -1, 0)
    far = [
        shift(up2[:cut], 1, 0, 0),
        shift(over_up[cut:cut2], 0, 1, 0),
        shift(over_down[cut2:], 0, -1, 0),
    ]
    mine = [value, down, up2, up, over, over_down, over_up] + far
    theirs = [shift(array, 0, 0, 1) for array in mine]
    pieces = []
    for side in range(2):
        at, pos = side * len(mine), side * len(NEAR)
        pieces += [(at + array, 0, rows, pos + position, 0) for array, position in enumerate([0, 1, 2, 3, 4, 5, 7])]
        pieces += [
            (at + 7, 0, cut, pos + 6, 0),
            (at + 8, 0, cut2 - cut, pos + 6, cut),
            (at + 9, 0, rows - cut2, pos + 6, cut2),
        ]
    return mine + theirs, pieces


def body(activations, gains, block_values, block_rows):
    first = lax.axis_index("pipe") == 0
    quarter = lax.axis_index("dp")
    here = lax.axis_index("tensor")
    gain = gains[0]
    own = activations.reshape(ROWS, WIDTH)
    with jax.named_scope("rows_first"):
        gathered = lax.all_gather(own, "tensor", axis=0, tiled=True)
    with jax.named_scope("gains"):
        all_gains = lax.all_to_all(jnp.broadcast_to(gain[None, :], (TENSOR, WIDTH)), "tensor", 0, 0, tiled=True)
        all_gains = all_gains[:, None, :]
    with jax.named_scope("weight"):
        weight = build_dense(block_values[0], block_rows[0])
    spot = jnp.stack([quarter, here // 8, here // 2 % 4, here % 2]).astype(jnp.int32)
    with jax.named_scope("layer_first"):
        pieces = [(0, block * ROWS, ROWS, block, 0) for block in range(TENSOR)]
        updated_first, _ = layer(spot, [gathered], pieces, weight, all_gains, own, True)
    with jax.named_scope("hand_over"):
        received = lax.ppermute(updated_first, "pipe", [(0, 1)])
    stream = jnp.where(first, own, received)
    with jax.named_scope("columns"):
        cols = lax.all_gather(jnp.where(first, own, 0) + received, "dp", axis=0)
    with jax.named_scope("rows_second"):
        arrays, pieces = gather_near(stream)
    with jax.named_scope("hessian_rows"):
        mine = len(arrays) // 2
        picked = pick(spot, arrays[:mine], [piece for piece in pieces if piece[0] < mine], cols)
        rows = [along_dp(picked[step], step) for step in range(1, DP)]
    with jax.named_scope("layer_second"):
        updated_second, stats = layer(spot, arrays, pieces, weight, all_gains, stream, False)
        stats = gather_dp(stats)
    with jax.named_scope("hessian"):
        near = [picked[0], *after(rows, [stats[0]])]
        far = [share(value, step) for step, value in enumerate(near) if step > 0]
        far[1:2] = after([far[1]], stats[1:])
        near += [shift(value, 0, 0, 1) for value in near]
        far += [shift(value, 0, 0, 1) for value in far]
        hessian = gram(spot, near, far, cols, stats, all_gains, gain[None, :])
    sections = jnp.where(first, updated_first, updated_second)
    return (hessian[None], sections.reshape(1, M, TOK, WIDTH))


def solution(mesh):
    return jax.shard_map(
        body,
        mesh=mesh,
        in_specs=(
            P(None, "dp", "tensor"),
            P("pipe", "tensor"),
            P("pipe", "tensor", None, None),
            P("pipe", "tensor", None),
        ),
        out_specs=(P("pipe", "dp", "tensor"), P("pipe", None, "dp", "tensor")),
        check_vma=False,
    )
```

```python
import jax
import jax.numpy as jnp
from jax import lax
from jax.experimental import pallas as pl
from jax.experimental.pallas import tpu as pltpu
from jax.sharding import PartitionSpec as P

D = 12288
BLOCK = 64
KEEP = 48
M = 4
TOK = 64
ROWS = M * TOK
DP = 4
TENSOR = 16
WIDTH = D // TENSOR
QUARTER = D // DP
EPSILON = 1e-05
LANES = 128
SPAN = 256
CHUNK = 64
MIB = 1024 * 1024
VMEM_LIMIT = 61 * MIB
NEAR = [(dz, dy) for dz in range(2) for dy in range(4)]
ANY = pl.BlockSpec(memory_space=pl.ANY)
VMEM = pl.BlockSpec(memory_space=pltpu.VMEM)
SMEM = pl.BlockSpec(memory_space=pltpu.SMEM)


def build_kernel(rows_ref, blocks_ref, dense_ref):
    group = pl.program_id(0)

    @pl.loop(0, D // SPAN)
    def _(chunk):
        dense_ref[0, pl.ds(pl.multiple_of(chunk * SPAN, SPAN), SPAN), :] = jnp.zeros((SPAN, SPAN), jnp.bfloat16)

    per = SPAN // BLOCK

    @pl.loop(0, KEEP, unroll=4)
    def _(kept):
        for part in range(per):
            first = pl.multiple_of(rows_ref[per * group + part, kept] * BLOCK, BLOCK)
            dense_ref[0, pl.ds(first, BLOCK), part * BLOCK:(part + 1) * BLOCK] = blocks_ref[part, kept]


def build_dense(values, rows_index):
    blocks = values.reshape(WIDTH // BLOCK, KEEP, BLOCK, BLOCK)
    per = SPAN // BLOCK
    return pl.pallas_call(
        build_kernel,
        grid_spec=pltpu.PrefetchScalarGridSpec(
            num_scalar_prefetch=1,
            grid=(WIDTH // SPAN,),
            in_specs=[pl.BlockSpec((per, KEEP, BLOCK, BLOCK), lambda group, rows: (group, 0, 0, 0))],
            out_specs=pl.BlockSpec((1, D, SPAN), lambda group, rows: (group, 0, 0)),
        ),
        out_shape=jax.ShapeDtypeStruct((WIDTH // SPAN, D, SPAN), jnp.bfloat16),
        compiler_params=pltpu.CompilerParams(vmem_limit_bytes=VMEM_LIMIT),
        cost_estimate=pl.CostEstimate(flops=0, bytes_accessed=32 * MIB, transcendentals=0),
        name="build_dense",
    )(rows_index, blocks)


def start_pieces(pieces, refs, rows, sems):
    for array, start, count, position, into in pieces:
        pltpu.make_async_copy(
            refs[array].at[pl.ds(start, count)], rows.at[position, pl.ds(into, count)], sems.at[position]
        ).start()


def wait_block(rows, sems, position):
    pltpu.make_async_copy(rows.at[position], rows.at[position], sems.at[position]).wait()


def spread(column, means, span):
    means[span] = jnp.broadcast_to(column, (ROWS, LANES))


def block_at(spot_ref, position):
    z = lax.rem(spot_ref[1] + lax.rem(position // 4, 2), 2)
    y = lax.rem(spot_ref[2] + lax.rem(position, 4), 4)
    core = lax.rem(spot_ref[3] + position // len(NEAR), 2)
    return z * 8 + y * 2 + core


def layer_kernel(pieces, count, straight, spot_ref, weight_ref, gains_ref, own_ref, *refs):
    sources, (out_ref, stats_ref, rows, weight, total, means, scales, sems, weight_sems) = refs[:count], refs[count:]

    def place(position):
        return position if straight else block_at(spot_ref, position)

    def weight_copy(position):
        span = pl.ds(pl.multiple_of(place(position) * WIDTH, WIDTH), WIDTH)
        into = pl.ds(pl.multiple_of(position * WIDTH, WIDTH), WIDTH)
        return pltpu.make_async_copy(weight_ref.at[:, span], weight.at[:, into], weight_sems.at[position])

    start_pieces(pieces, sources, rows, sems)
    means[...] = jnp.zeros_like(means)
    scales[...] = jnp.zeros_like(scales)
    total[...] = own_ref[...].astype(jnp.float32)
    @pl.loop(0, TENSOR // 2)
    def _(pair):
        for position in (2 * pair, 2 * pair + 1):
            wait_block(rows, sems, position)
            for chunk in range(0, ROWS, CHUNK):
                span = slice(chunk, chunk + CHUNK)
                added = jnp.zeros((CHUNK, LANES), jnp.float32)
                squared = added
                for part in range(WIDTH // LANES):
                    values = rows[position, span, part * LANES:(part + 1) * LANES].astype(jnp.float32)
                    added = added + values
                    squared = squared + values * values
                means[span] += added
                scales[span] += squared
        weight_copy(pair).start()

    mean = jnp.sum(means[...], axis=1, keepdims=True) / D
    square = jnp.sum(scales[...], axis=1, keepdims=True) / D
    scale = lax.rsqrt(square - mean * mean + EPSILON)
    lane = lax.broadcasted_iota(jnp.int32, (ROWS, LANES), 1)
    stats_ref[...] = jnp.transpose(jnp.where(lane == 0, mean, scale))[:8]
    spread(mean, means, slice(0, ROWS))
    spread(scale, scales, slice(0, ROWS))

    def normalise(position):
        gain = gains_ref[place(position)]
        for chunk in range(0, ROWS, CHUNK):
            span = slice(chunk, chunk + CHUNK)
            for part in range(WIDTH // LANES):
                lanes = slice(part * LANES, (part + 1) * LANES)
                values = rows[position, span, lanes].astype(jnp.float32)
                scaled = (values - means[span]) * scales[span] * gain[:, lanes]
                rows[position, span, lanes] = scaled.astype(jnp.bfloat16)

    normalise(0)
    normalise(1)

    @pl.loop(0, TENSOR // 2)
    def _(pair):
        position = 2 * pair
        for later in range(2):

            @pl.when(position + TENSOR // 2 + later < TENSOR)
            def _():
                weight_copy(position + TENSOR // 2 + later).start()

        weight_copy(position).wait()
        weight_copy(position + 1).wait()
        left = jnp.concatenate([rows[position], rows[position + 1]], axis=1)
        span = pl.ds(pl.multiple_of(position * WIDTH, 2 * WIDTH), 2 * WIDTH)
        for group in range(WIDTH // SPAN):
            lanes = slice(group * SPAN, (group + 1) * SPAN)
            total[:, lanes] += jnp.dot(left, weight[group, span], preferred_element_type=jnp.float32)

        @pl.when(position + 2 < TENSOR)
        def _():
            normalise(position + 2)
            normalise(position + 3)

    out_ref[...] = total[...].astype(jnp.bfloat16)


def in_hbm(arrays):
    return [pltpu.with_memory_space_constraint(array, pltpu.HBM) for array in arrays]


def layer(spot, gathered, pieces, weight, gains, own, straight):
    count = len(gathered)
    return pl.pallas_call(
        lambda *refs: layer_kernel(pieces, count, straight, *refs),
        in_specs=[SMEM, ANY, VMEM, VMEM] + [ANY] * count,
        out_specs=[VMEM, VMEM],
        out_shape=[
            jax.ShapeDtypeStruct((ROWS, WIDTH), jnp.bfloat16),
            jax.ShapeDtypeStruct((8, ROWS), jnp.float32),
        ],
        scratch_shapes=[
            pltpu.VMEM((TENSOR, ROWS, WIDTH), jnp.bfloat16),
            pltpu.VMEM((WIDTH // SPAN, D, SPAN), jnp.bfloat16),
            pltpu.VMEM((ROWS, WIDTH), jnp.float32),
            pltpu.VMEM((ROWS, LANES), jnp.float32),
            pltpu.VMEM((ROWS, LANES), jnp.float32),
            pltpu.SemaphoreType.DMA((TENSOR,)),
            pltpu.SemaphoreType.DMA((TENSOR,)),
        ],
        compiler_params=pltpu.CompilerParams(vmem_limit_bytes=VMEM_LIMIT),
        cost_estimate=pl.CostEstimate(flops=2 * ROWS * D * WIDTH, bytes_accessed=2 * D * (WIDTH + ROWS), transcendentals=ROWS),
        name="layer",
    )(spot, *in_hbm([weight]), gains, own, *in_hbm(gathered))


PIECE = 384
PER = WIDTH // PIECE
HALF = TENSOR // DP // 2
CLASSES = [(side, half) for side in range(2) for half in range(HALF)]


def half_at(spot_ref, step):
    return spot_ref[1] if step == 2 else lax.rem(spot_ref[2], 2)


def pick_kernel(pieces, count, spot_ref, *refs):
    sources, picked, sems = refs[:count], refs[count + 1:-1], refs[-1]
    jobs = [(0, 0, 0), (0, 1, 1)] + [(step, half_at(spot_ref, step), 0) for step in range(1, DP)]
    for job, (step, half, into) in enumerate(jobs):
        target = lax.rem(spot_ref[0] + step, DP)
        dz = lax.rem(target // 2 + 2 - spot_ref[1], 2)
        dy = lax.rem(lax.rem(target, 2) * 2 + half + 4 - spot_ref[2], 4)
        for position in range(len(NEAR)):

            @pl.when(dz * 4 + dy == position)
            def _():
                for array, start, size, at, row in pieces:
                    if at == position:
                        pltpu.make_async_copy(
                            sources[array].at[pl.ds(start, size)],
                            picked[step].at[pl.ds(into * ROWS + row, size)],
                            sems.at[job],
                        ).start()

    for job, (step, _, into) in enumerate(jobs):
        block = picked[step].at[pl.ds(into * ROWS, ROWS)]
        pltpu.make_async_copy(block, block, sems.at[job]).wait()


def pick(spot, gathered, pieces, before):
    count = len(gathered)
    return pl.pallas_call(
        lambda *refs: pick_kernel(pieces, count, *refs),
        in_specs=[SMEM] + [ANY] * (count + 1),
        out_specs=[VMEM] * DP,
        out_shape=[jax.ShapeDtypeStruct((rows, WIDTH), jnp.bfloat16) for rows in [HALF * ROWS] + [ROWS] * (DP - 1)],
        scratch_shapes=[pltpu.SemaphoreType.DMA((DP + 1,))],
        compiler_params=pltpu.CompilerParams(vmem_limit_bytes=VMEM_LIMIT),
        cost_estimate=pl.CostEstimate(flops=0, bytes_accessed=4 * (DP + 1) * ROWS * WIDTH, transcendentals=0),
        name="pick",
    )(spot, *in_hbm(gathered), before)


def after(values, others):
    count = len(values)
    return pl.pallas_call(
        lambda *refs: None,
        in_specs=[ANY] * (count + len(others)),
        out_specs=[ANY] * count,
        out_shape=[jax.ShapeDtypeStruct(value.shape, value.dtype) for value in values],
        input_output_aliases={place: place for place in range(count)},
        name="after",
    )(*in_hbm(values), *others)


def gram_kernel(spot_ref, *refs):
    near, far, refs = refs[:2 * DP], refs[2 * DP:4 * DP - 2], refs[4 * DP - 2:]
    stats_refs, refs = refs[:DP], refs[DP:]
    cols_ref, gains_ref, col_gain_ref, out_ref, rows, cols, means, scales, left, result, sems, row_sems = refs

    def block_of(group):
        return lax.rem(spot_ref[3] + group // HALF, 2) + 2 * lax.rem(group, HALF)

    def row_copy(source, group, part):
        return pltpu.make_async_copy(source, rows.at[group, part], row_sems.at[group, part])

    def start_rows(side):
        for half in range(HALF):
            row_copy(near[side * DP].at[pl.ds(half * ROWS, ROWS)], side * HALF + half, 0).start()
        for part in range(1, DP):
            half = half_at(spot_ref, part)
            row_copy(near[side * DP + part], side * HALF + half, part).start()
            row_copy(far[side * (DP - 1) + part - 1], side * HALF + 1 - half, part).start()

    start_rows(0)
    for part in range(DP):
        span = slice(part * ROWS, (part + 1) * ROWS)
        means[span] = jnp.transpose(jnp.broadcast_to(stats_refs[part][0:1], (LANES, ROWS)))
        scales[span] = jnp.transpose(jnp.broadcast_to(stats_refs[part][1:2], (LANES, ROWS)))
        for chunk in range(0, ROWS, CHUNK):
            span = slice(part * ROWS + chunk, part * ROWS + chunk + CHUNK)
            for lane in range(WIDTH // LANES):
                lanes = slice(lane * LANES, (lane + 1) * LANES)
                values = cols_ref[lax.rem(spot_ref[0] + DP - part, DP), chunk:chunk + CHUNK, lanes].astype(jnp.float32)
                scaled = (values - means[span]) * scales[span] * col_gain_ref[:, lanes]
                cols[span, lanes] = scaled.astype(jnp.bfloat16)

    def normalise(group, slot):
        if slot == 0:
            for part in range(DP):
                row_copy(rows.at[group, part], group, part).wait()
        gain = gains_ref[spot_ref[0] * (TENSOR // DP) + block_of(group)]
        for part in range(DP):
            for chunk in range(0, ROWS, CHUNK):
                span = slice(part * ROWS + chunk, part * ROWS + chunk + CHUNK)
                for lane in range(PIECE // LANES):
                    first = slot * PIECE + lane * LANES
                    from_lanes = slice(first, first + LANES)
                    values = rows[group, part, chunk:chunk + CHUNK, from_lanes].astype(jnp.float32)
                    scaled = (values - means[span]) * scales[span] * gain[:, from_lanes]
                    left[slot, span, lane * LANES:(lane + 1) * LANES] = scaled.astype(jnp.bfloat16)

    def store(group, slot):
        row = pl.multiple_of(block_of(group) * WIDTH + slot * PIECE, PIECE)
        return pltpu.make_async_copy(result.at[slot], out_ref.at[pl.ds(row, PIECE)], sems.at[slot])

    normalise(0, 0)
    start_rows(1)

    @pl.loop(0, len(CLASSES))
    def _(group):
        for slot in range(PER):
            product = lax.dot_general(
                left[slot], cols[...], (((0,), (0,)), ((), ())), preferred_element_type=jnp.float32
            )

            @pl.when(group > 0)
            def _():
                store(group - 1, slot).wait()

            result[slot] = product * (2.0 / (DP * ROWS))
            store(group, slot).start()
            if slot + 1 < PER:
                normalise(group, slot + 1)
            else:

                @pl.when(group + 1 < len(CLASSES))
                def _():
                    normalise(group + 1, 0)

    for slot in range(PER):
        store(len(CLASSES) - 1, slot).wait()


def gram(spot, near, far, cols, stats, gains, col_gain):
    return pl.pallas_call(
        gram_kernel,
        in_specs=[SMEM] + [ANY] * (4 * DP - 2) + [VMEM] * (DP + 3),
        out_specs=ANY,
        out_shape=jax.ShapeDtypeStruct((QUARTER, WIDTH), jnp.float32),
        scratch_shapes=[
            pltpu.VMEM((len(CLASSES), DP, ROWS, WIDTH), jnp.bfloat16),
            pltpu.VMEM((DP * ROWS, WIDTH), jnp.bfloat16),
            pltpu.VMEM((DP * ROWS, LANES), jnp.float32),
            pltpu.VMEM((DP * ROWS, LANES), jnp.float32),
            pltpu.VMEM((2, DP * ROWS, PIECE), jnp.bfloat16),
            pltpu.VMEM((2, PIECE, WIDTH), jnp.float32),
            pltpu.SemaphoreType.DMA((2,)),
            pltpu.SemaphoreType.DMA((len(CLASSES), DP)),
        ],
        compiler_params=pltpu.CompilerParams(vmem_limit_bytes=VMEM_LIMIT),
        cost_estimate=pl.CostEstimate(
            flops=2 * DP * ROWS * QUARTER * WIDTH, bytes_accessed=4 * QUARTER * WIDTH + 2 * DP * ROWS * (QUARTER + WIDTH), transcendentals=0
        ),
        name="gram",
    )(spot, *near, *far, *stats, cols, gains, col_gain)


def along_dp(value, step):
    return lax.ppermute(value, "dp", [(source, (source + step) % DP) for source in range(DP)])


def gather_dp(value):
    return [value] + [along_dp(value, step) for step in range(1, DP)]


def tensor_at(z, y, core):
    return (z % 2) * 8 + (y % 4) * 2 + core % 2


def shift(value, z, y, core):
    pairs = [
        (tensor_at(a, b, c), tensor_at(a + z, b + y, c + core)) for a in range(2) for b in range(4) for c in range(2)
    ]
    return lax.ppermute(value, "tensor", pairs)


def share(value, step):
    pairs = []
    for z in range(2):
        for y in range(4):
            for core in range(2):
                to = {1: (z, y ^ 1), 2: (1 - z, y), 3: (z, 3 - y)}[step]
                pairs.append((tensor_at(z, y, core), tensor_at(*to, core)))
    return lax.ppermute(value, "tensor", pairs)


def gather_near(value):
    rows = value.shape[0]
    cut, cut2 = rows * 3 // 8, rows * 11 // 16
    up, down, over = shift(value, 0, 1, 0), shift(value, 0, -1, 0), shift(value, 1, 0, 0)
    up2, over_up, over_down = shift(up, 0, 1, 0), shift(up, 1, 0, 0), shift(over, 0, -1, 0)
    far = [
        shift(up2[:cut], 1, 0, 0),
        shift(over_up[cut:cut2], 0, 1, 0),
        shift(over_down[cut2:], 0, -1, 0),
    ]
    mine = [value, down, up2, up, over, over_down, over_up] + far
    theirs = [shift(array, 0, 0, 1) for array in mine]
    pieces = []
    for side in range(2):
        at, pos = side * len(mine), side * len(NEAR)
        pieces += [(at + array, 0, rows, pos + position, 0) for array, position in enumerate([0, 1, 2, 3, 4, 5, 7])]
        pieces += [
            (at + 7, 0, cut, pos + 6, 0),
            (at + 8, 0, cut2 - cut, pos + 6, cut),
            (at + 9, 0, rows - cut2, pos + 6, cut2),
        ]
    return mine + theirs, pieces


def body(activations, gains, block_values, block_rows):
    first = lax.axis_index("pipe") == 0
    quarter = lax.axis_index("dp")
    here = lax.axis_index("tensor")
    gain = gains[0]
    own = activations.reshape(ROWS, WIDTH)
    with jax.named_scope("rows_first"):
        gathered = lax.all_gather(own, "tensor", axis=0, tiled=True)
    with jax.named_scope("gains"):
        all_gains = lax.all_to_all(jnp.broadcast_to(gain[None, :], (TENSOR, WIDTH)), "tensor", 0, 0, tiled=True)
        all_gains = all_gains[:, None, :]
    with jax.named_scope("weight"):
        weight = build_dense(block_values[0], block_rows[0])
    spot = jnp.stack([quarter, here // 8, here // 2 % 4, here % 2]).astype(jnp.int32)
    with jax.named_scope("layer_first"):
        pieces = [(0, block * ROWS, ROWS, block, 0) for block in range(TENSOR)]
        updated_first, _ = layer(spot, [gathered], pieces, weight, all_gains, own, True)
    with jax.named_scope("hand_over"):
        received = lax.ppermute(updated_first, "pipe", [(0, 1)])
    stream = jnp.where(first, own, received)
    with jax.named_scope("columns"):
        cols = lax.all_gather(jnp.where(first, own, 0) + received, "dp", axis=0)
    with jax.named_scope("rows_second"):
        arrays, pieces = gather_near(stream)
    with jax.named_scope("hessian_rows"):
        mine = len(arrays) // 2
        picked = pick(spot, arrays[:mine], [piece for piece in pieces if piece[0] < mine], cols)
        rows = [along_dp(picked[step], step) for step in range(1, DP)]
    with jax.named_scope("layer_second"):
        updated_second, stats = layer(spot, arrays, pieces, weight, all_gains, stream, False)
        stats = gather_dp(stats)
    with jax.named_scope("hessian"):
        near = [picked[0], *after(rows, [stats[0]])]
        far = [share(value, step) for step, value in enumerate(near) if step > 0]
        far[1:2] = after([far[1]], stats[1:])
        near += [shift(value, 0, 0, 1) for value in near]
        far += [shift(value, 0, 0, 1) for value in far]
        hessian = gram(spot, near, far, cols, stats, all_gains, gain[None, :])
    sections = jnp.where(first, updated_first, updated_second)
    return (hessian[None], sections.reshape(1, M, TOK, WIDTH))


def solution(mesh):
    return jax.shard_map(
        body,
        mesh=mesh,
        in_specs=(
            P(None, "dp", "tensor"),
            P("pipe", "tensor"),
            P("pipe", "tensor", None, None),
            P("pipe", "tensor", None),
        ),
        out_specs=(P("pipe", "dp", "tensor"), P("pipe", None, "dp", "tensor")),
        check_vma=False,
    )
```

```python
import jax
import jax.numpy as jnp
from jax import lax
from jax.experimental import pallas as pl
from jax.experimental.pallas import tpu as pltpu
from jax.sharding import PartitionSpec as P

D = 12288
BLOCK = 64
KEEP = 48
M = 4
TOK = 64
ROWS = M * TOK
DP = 4
TENSOR = 16
WIDTH = D // TENSOR
QUARTER = D // DP
EPSILON = 1e-05
LANES = 128
SPAN = 256
CHUNK = 64
MIB = 1024 * 1024
VMEM_LIMIT = 61 * MIB
NEAR = [(dz, dy) for dz in range(2) for dy in range(4)]
ANY = pl.BlockSpec(memory_space=pl.ANY)
VMEM = pl.BlockSpec(memory_space=pltpu.VMEM)
SMEM = pl.BlockSpec(memory_space=pltpu.SMEM)


def build_kernel(rows_ref, blocks_ref, dense_ref):
    group = pl.program_id(0)

    @pl.loop(0, D // SPAN)
    def _(chunk):
        dense_ref[0, pl.ds(pl.multiple_of(chunk * SPAN, SPAN), SPAN), :] = jnp.zeros((SPAN, SPAN), jnp.bfloat16)

    per = SPAN // BLOCK

    @pl.loop(0, KEEP, unroll=4)
    def _(kept):
        for part in range(per):
            first = pl.multiple_of(rows_ref[per * group + part, kept] * BLOCK, BLOCK)
            dense_ref[0, pl.ds(first, BLOCK), part * BLOCK:(part + 1) * BLOCK] = blocks_ref[part, kept]


def build_dense(values, rows_index):
    blocks = values.reshape(WIDTH // BLOCK, KEEP, BLOCK, BLOCK)
    per = SPAN // BLOCK
    return pl.pallas_call(
        build_kernel,
        grid_spec=pltpu.PrefetchScalarGridSpec(
            num_scalar_prefetch=1,
            grid=(WIDTH // SPAN,),
            in_specs=[pl.BlockSpec((per, KEEP, BLOCK, BLOCK), lambda group, rows: (group, 0, 0, 0))],
            out_specs=pl.BlockSpec((1, D, SPAN), lambda group, rows: (group, 0, 0)),
        ),
        out_shape=jax.ShapeDtypeStruct((WIDTH // SPAN, D, SPAN), jnp.bfloat16),
        compiler_params=pltpu.CompilerParams(vmem_limit_bytes=VMEM_LIMIT),
        cost_estimate=pl.CostEstimate(flops=0, bytes_accessed=32 * MIB, transcendentals=0),
        name="build_dense",
    )(rows_index, blocks)


def start_pieces(pieces, refs, rows, sems):
    for array, start, count, position, into in pieces:
        pltpu.make_async_copy(
            refs[array].at[pl.ds(start, count)], rows.at[position, pl.ds(into, count)], sems.at[position]
        ).start()


def wait_block(rows, sems, position):
    pltpu.make_async_copy(rows.at[position], rows.at[position], sems.at[position]).wait()


def spread(column, means, span):
    means[span] = jnp.broadcast_to(column, (ROWS, LANES))


def block_at(spot_ref, position):
    z = lax.rem(spot_ref[1] + lax.rem(position // 4, 2), 2)
    y = lax.rem(spot_ref[2] + lax.rem(position, 4), 4)
    core = lax.rem(spot_ref[3] + position // len(NEAR), 2)
    return z * 8 + y * 2 + core


def layer_kernel(pieces, count, straight, spot_ref, weight_ref, gains_ref, own_ref, *refs):
    if not straight:
        earlier_ref, refs = refs[0], refs[1:]
    sources, (out_ref, stats_ref, rows, weight, total, means, scales, sems, weight_sems) = refs[:count], refs[count:]

    def place(position):
        return position if straight else block_at(spot_ref, position)

    def weight_copy(position):
        span = pl.ds(pl.multiple_of(place(position) * WIDTH, WIDTH), WIDTH)
        into = pl.ds(pl.multiple_of(position * WIDTH, WIDTH), WIDTH)
        return pltpu.make_async_copy(weight_ref.at[:, span], weight.at[:, into], weight_sems.at[position])

    start_pieces(pieces, sources, rows, sems)
    means[...] = jnp.zeros_like(means)
    scales[...] = jnp.zeros_like(scales)
    total[...] = own_ref[...].astype(jnp.float32)
    @pl.loop(0, TENSOR // 2)
    def _(pair):
        for position in (2 * pair, 2 * pair + 1):
            wait_block(rows, sems, position)
            for chunk in range(0, ROWS, CHUNK):
                span = slice(chunk, chunk + CHUNK)
                added = jnp.zeros((CHUNK, LANES), jnp.float32)
                squared = added
                for part in range(WIDTH // LANES):
                    values = rows[position, span, part * LANES:(part + 1) * LANES].astype(jnp.float32)
                    added = added + values
                    squared = squared + values * values
                means[span] += added
                scales[span] += squared
        weight_copy(pair).start()

    mean = jnp.sum(means[...], axis=1, keepdims=True) / D
    square = jnp.sum(scales[...], axis=1, keepdims=True) / D
    scale = lax.rsqrt(square - mean * mean + EPSILON)
    lane = lax.broadcasted_iota(jnp.int32, (ROWS, LANES), 1)
    stats_ref[...] = jnp.transpose(jnp.where(lane == 0, mean, scale))[:8]
    spread(mean, means, slice(0, ROWS))
    spread(scale, scales, slice(0, ROWS))

    def normalise(position):
        gain = gains_ref[place(position)]
        for chunk in range(0, ROWS, CHUNK):
            span = slice(chunk, chunk + CHUNK)
            for part in range(WIDTH // LANES):
                lanes = slice(part * LANES, (part + 1) * LANES)
                values = rows[position, span, lanes].astype(jnp.float32)
                scaled = (values - means[span]) * scales[span] * gain[:, lanes]
                rows[position, span, lanes] = scaled.astype(jnp.bfloat16)

    normalise(0)
    normalise(1)

    @pl.loop(0, TENSOR // 2)
    def _(pair):
        position = 2 * pair
        for later in range(2):

            @pl.when(position + TENSOR // 2 + later < TENSOR)
            def _():
                weight_copy(position + TENSOR // 2 + later).start()

        weight_copy(position).wait()
        weight_copy(position + 1).wait()
        left = jnp.concatenate([rows[position], rows[position + 1]], axis=1)
        span = pl.ds(pl.multiple_of(position * WIDTH, 2 * WIDTH), 2 * WIDTH)
        for group in range(WIDTH // SPAN):
            lanes = slice(group * SPAN, (group + 1) * SPAN)
            total[:, lanes] += jnp.dot(left, weight[group, span], preferred_element_type=jnp.float32)

        @pl.when(position + 2 < TENSOR)
        def _():
            normalise(position + 2)
            normalise(position + 3)

    out_ref[...] = total[...].astype(jnp.bfloat16)
    if not straight:

        @pl.when(spot_ref[4] == 0)
        def _():
            out_ref[...] = earlier_ref[...]


def in_hbm(arrays):
    return [pltpu.with_memory_space_constraint(array, pltpu.HBM) for array in arrays]


def layer(spot, gathered, pieces, weight, gains, own, earlier=None):
    count, straight = len(gathered), earlier is None
    return pl.pallas_call(
        lambda *refs: layer_kernel(pieces, count, straight, *refs),
        in_specs=[SMEM, ANY, VMEM, VMEM] + [VMEM] * (not straight) + [ANY] * count,
        out_specs=[VMEM, VMEM],
        out_shape=[
            jax.ShapeDtypeStruct((ROWS, WIDTH), jnp.bfloat16),
            jax.ShapeDtypeStruct((8, ROWS), jnp.float32),
        ],
        scratch_shapes=[
            pltpu.VMEM((TENSOR, ROWS, WIDTH), jnp.bfloat16),
            pltpu.VMEM((WIDTH // SPAN, D, SPAN), jnp.bfloat16),
            pltpu.VMEM((ROWS, WIDTH), jnp.float32),
            pltpu.VMEM((ROWS, LANES), jnp.float32),
            pltpu.VMEM((ROWS, LANES), jnp.float32),
            pltpu.SemaphoreType.DMA((TENSOR,)),
            pltpu.SemaphoreType.DMA((TENSOR,)),
        ],
        compiler_params=pltpu.CompilerParams(vmem_limit_bytes=VMEM_LIMIT),
        cost_estimate=pl.CostEstimate(flops=2 * ROWS * D * WIDTH, bytes_accessed=2 * D * (WIDTH + ROWS), transcendentals=ROWS),
        name="layer",
    )(spot, *in_hbm([weight]), gains, own, *([] if straight else [earlier]), *in_hbm(gathered))


PIECE = 384
PER = WIDTH // PIECE
HALF = TENSOR // DP // 2
CLASSES = [(side, half) for side in range(2) for half in range(HALF)]


def half_at(spot_ref, step):
    return spot_ref[1] if step == 2 else lax.rem(spot_ref[2], 2)


def pick_kernel(pieces, count, spot_ref, *refs):
    sources, picked, sems = refs[:count], refs[count + 1:-1], refs[-1]
    jobs = [(0, 0, 0), (0, 1, 1)] + [(step, half_at(spot_ref, step), 0) for step in range(1, DP)]
    for job, (step, half, into) in enumerate(jobs):
        target = lax.rem(spot_ref[0] + step, DP)
        dz = lax.rem(target // 2 + 2 - spot_ref[1], 2)
        dy = lax.rem(lax.rem(target, 2) * 2 + half + 4 - spot_ref[2], 4)
        for position in range(len(NEAR)):

            @pl.when(dz * 4 + dy == position)
            def _():
                for array, start, size, at, row in pieces:
                    if at == position:
                        pltpu.make_async_copy(
                            sources[array].at[pl.ds(start, size)],
                            picked[step].at[pl.ds(into * ROWS + row, size)],
                            sems.at[job],
                        ).start()

    for job, (step, _, into) in enumerate(jobs):
        block = picked[step].at[pl.ds(into * ROWS, ROWS)]
        pltpu.make_async_copy(block, block, sems.at[job]).wait()


def pick(spot, gathered, pieces, before):
    count = len(gathered)
    return pl.pallas_call(
        lambda *refs: pick_kernel(pieces, count, *refs),
        in_specs=[SMEM] + [ANY] * (count + 1),
        out_specs=[VMEM] * DP,
        out_shape=[jax.ShapeDtypeStruct((rows, WIDTH), jnp.bfloat16) for rows in [HALF * ROWS] + [ROWS] * (DP - 1)],
        scratch_shapes=[pltpu.SemaphoreType.DMA((DP + 1,))],
        compiler_params=pltpu.CompilerParams(vmem_limit_bytes=VMEM_LIMIT),
        cost_estimate=pl.CostEstimate(flops=0, bytes_accessed=4 * (DP + 1) * ROWS * WIDTH, transcendentals=0),
        name="pick",
    )(spot, *in_hbm(gathered), before)


def after(values, others):
    count = len(values)
    return pl.pallas_call(
        lambda *refs: None,
        in_specs=[ANY] * (count + len(others)),
        out_specs=[ANY] * count,
        out_shape=[jax.ShapeDtypeStruct(value.shape, value.dtype) for value in values],
        input_output_aliases={place: place for place in range(count)},
        name="after",
    )(*in_hbm(values), *others)


def gram_kernel(spot_ref, *refs):
    near, far, refs = refs[:2 * DP], refs[2 * DP:4 * DP - 2], refs[4 * DP - 2:]
    stats_refs, refs = refs[:DP], refs[DP:]
    cols_ref, gains_ref, col_gain_ref, out_ref, rows, given, cols, means, scales, left, result, sems, row_sems, col_sem = refs

    def block_of(group):
        return lax.rem(spot_ref[3] + group // HALF, 2) + 2 * lax.rem(group, HALF)

    def row_copy(source, group, part):
        return pltpu.make_async_copy(source, rows.at[group, part], row_sems.at[group, part])

    def start_rows(side):
        for half in range(HALF):
            row_copy(near[side * DP].at[pl.ds(half * ROWS, ROWS)], side * HALF + half, 0).start()
        for part in range(1, DP):
            half = half_at(spot_ref, part)
            row_copy(near[side * DP + part], side * HALF + half, part).start()
            row_copy(far[side * (DP - 1) + part - 1], side * HALF + 1 - half, part).start()

    columns = pltpu.make_async_copy(cols_ref, given, col_sem)
    columns.start()
    start_rows(0)
    for part in range(DP):
        span = slice(part * ROWS, (part + 1) * ROWS)
        means[span] = jnp.transpose(jnp.broadcast_to(stats_refs[part][0:1], (LANES, ROWS)))
        scales[span] = jnp.transpose(jnp.broadcast_to(stats_refs[part][1:2], (LANES, ROWS)))
    columns.wait()
    for part in range(DP):
        for chunk in range(0, ROWS, CHUNK):
            span = slice(part * ROWS + chunk, part * ROWS + chunk + CHUNK)
            for lane in range(WIDTH // LANES):
                lanes = slice(lane * LANES, (lane + 1) * LANES)
                values = given[lax.rem(spot_ref[0] + DP - part, DP), chunk:chunk + CHUNK, lanes].astype(jnp.float32)
                scaled = (values - means[span]) * scales[span] * col_gain_ref[:, lanes]
                cols[span, lanes] = scaled.astype(jnp.bfloat16)

    def normalise(group, slot):
        if slot == 0:
            for part in range(DP):
                row_copy(rows.at[group, part], group, part).wait()
        gain = gains_ref[spot_ref[0] * (TENSOR // DP) + block_of(group)]
        for part in range(DP):
            for chunk in range(0, ROWS, CHUNK):
                span = slice(part * ROWS + chunk, part * ROWS + chunk + CHUNK)
                for lane in range(PIECE // LANES):
                    first = slot * PIECE + lane * LANES
                    from_lanes = slice(first, first + LANES)
                    values = rows[group, part, chunk:chunk + CHUNK, from_lanes].astype(jnp.float32)
                    scaled = (values - means[span]) * scales[span] * gain[:, from_lanes]
                    left[slot, span, lane * LANES:(lane + 1) * LANES] = scaled.astype(jnp.bfloat16)

    def store(group, slot):
        row = pl.multiple_of(block_of(group) * WIDTH + slot * PIECE, PIECE)
        return pltpu.make_async_copy(result.at[slot], out_ref.at[pl.ds(row, PIECE)], sems.at[slot])

    normalise(0, 0)
    start_rows(1)

    for group in range(len(CLASSES)):
        for slot in range(PER):
            product = lax.dot_general(
                left[slot], cols[...], (((0,), (0,)), ((), ())), preferred_element_type=jnp.float32
            )
            if group > 0:
                store(group - 1, slot).wait()
            result[slot] = product * (2.0 / (DP * ROWS))
            store(group, slot).start()
            if slot + 1 < PER:
                normalise(group, slot + 1)
            elif group + 1 < len(CLASSES):
                normalise(group + 1, 0)

    for slot in range(PER):
        store(len(CLASSES) - 1, slot).wait()


def gram(spot, near, far, cols, stats, gains, col_gain):
    return pl.pallas_call(
        gram_kernel,
        in_specs=[SMEM] + [ANY] * (4 * DP - 2) + [VMEM] * DP + [ANY, VMEM, VMEM],
        out_specs=ANY,
        out_shape=jax.ShapeDtypeStruct((QUARTER, WIDTH), jnp.float32),
        scratch_shapes=[
            pltpu.VMEM((len(CLASSES), DP, ROWS, WIDTH), jnp.bfloat16),
            pltpu.VMEM((DP, ROWS, WIDTH), jnp.bfloat16),
            pltpu.VMEM((DP * ROWS, WIDTH), jnp.bfloat16),
            pltpu.VMEM((DP * ROWS, LANES), jnp.float32),
            pltpu.VMEM((DP * ROWS, LANES), jnp.float32),
            pltpu.VMEM((2, DP * ROWS, PIECE), jnp.bfloat16),
            pltpu.VMEM((2, PIECE, WIDTH), jnp.float32),
            pltpu.SemaphoreType.DMA((2,)),
            pltpu.SemaphoreType.DMA((len(CLASSES), DP)),
            pltpu.SemaphoreType.DMA(()),
        ],
        compiler_params=pltpu.CompilerParams(vmem_limit_bytes=VMEM_LIMIT),
        cost_estimate=pl.CostEstimate(
            flops=2 * DP * ROWS * QUARTER * WIDTH, bytes_accessed=4 * QUARTER * WIDTH + 2 * DP * ROWS * (QUARTER + WIDTH), transcendentals=0
        ),
        name="gram",
    )(spot, *near, *far, *stats, *in_hbm([cols]), gains, col_gain)


def along_dp(value, step):
    return lax.ppermute(value, "dp", [(source, (source + step) % DP) for source in range(DP)])


def gather_dp(value):
    return [value] + [along_dp(value, step) for step in range(1, DP)]


def tensor_at(z, y, core):
    return (z % 2) * 8 + (y % 4) * 2 + core % 2


def shift(value, z, y, core):
    pairs = [
        (tensor_at(a, b, c), tensor_at(a + z, b + y, c + core)) for a in range(2) for b in range(4) for c in range(2)
    ]
    return lax.ppermute(value, "tensor", pairs)


def share(value, step):
    pairs = []
    for z in range(2):
        for y in range(4):
            for core in range(2):
                to = {1: (z, y ^ 1), 2: (1 - z, y), 3: (z, 3 - y)}[step]
                pairs.append((tensor_at(z, y, core), tensor_at(*to, core)))
    return lax.ppermute(value, "tensor", pairs)


def gather_near(value):
    rows = value.shape[0]
    cut, cut2 = rows * 3 // 8, rows * 11 // 16
    up, down, over = shift(value, 0, 1, 0), shift(value, 0, -1, 0), shift(value, 1, 0, 0)
    up2, over_up, over_down = shift(up, 0, 1, 0), shift(up, 1, 0, 0), shift(over, 0, -1, 0)
    far = [
        shift(up2[:cut], 1, 0, 0),
        shift(over_up[cut:cut2], 0, 1, 0),
        shift(over_down[cut2:], 0, -1, 0),
    ]
    mine = [value, down, up2, up, over, over_down, over_up] + far
    theirs = [shift(array, 0, 0, 1) for array in mine]
    pieces = []
    for side in range(2):
        at, pos = side * len(mine), side * len(NEAR)
        pieces += [(at + array, 0, rows, pos + position, 0) for array, position in enumerate([0, 1, 2, 3, 4, 5, 7])]
        pieces += [
            (at + 7, 0, cut, pos + 6, 0),
            (at + 8, 0, cut2 - cut, pos + 6, cut),
            (at + 9, 0, rows - cut2, pos + 6, cut2),
        ]
    return mine + theirs, pieces


def body(activations, gains, block_values, block_rows):
    first = lax.axis_index("pipe") == 0
    quarter = lax.axis_index("dp")
    here = lax.axis_index("tensor")
    gain = gains[0]
    own = activations.reshape(ROWS, WIDTH)
    with jax.named_scope("rows_first"):
        gathered = lax.all_gather(own, "tensor", axis=0, tiled=True)
    with jax.named_scope("gains"):
        all_gains = lax.all_to_all(jnp.broadcast_to(gain[None, :], (TENSOR, WIDTH)), "tensor", 0, 0, tiled=True)
        all_gains = all_gains[:, None, :]
    with jax.named_scope("weight"):
        weight = build_dense(block_values[0], block_rows[0])
    spot = jnp.stack([quarter, here // 8, here // 2 % 4, here % 2, lax.axis_index("pipe")]).astype(jnp.int32)
    with jax.named_scope("layer_first"):
        pieces = [(0, block * ROWS, ROWS, block, 0) for block in range(TENSOR)]
        updated_first, _ = layer(spot, [gathered], pieces, weight, all_gains, own)
    with jax.named_scope("hand_over"):
        received = lax.ppermute(updated_first, "pipe", [(0, 1)])
    stream = jnp.where(first, own, received)
    with jax.named_scope("columns"):
        cols = lax.all_gather(jnp.where(first, own, 0) + received, "dp", axis=0)
    with jax.named_scope("rows_second"):
        arrays, pieces = gather_near(stream)
    with jax.named_scope("hessian_rows"):
        mine = len(arrays) // 2
        picked = pick(spot, arrays[:mine], [piece for piece in pieces if piece[0] < mine], cols)
        rows = [along_dp(picked[step], step) for step in range(1, DP)]
    with jax.named_scope("layer_second"):
        sections, stats = layer(spot, arrays, pieces, weight, all_gains, stream, updated_first)
        stats = gather_dp(stats)
    with jax.named_scope("hessian"):
        near = [picked[0], *after(rows, [stats[0]])]
        far = [share(value, step) for step, value in enumerate(near) if step > 0]
        far[1:2] = after([far[1]], stats[1:])
        near += [shift(value, 0, 0, 1) for value in near]
        far += [shift(value, 0, 0, 1) for value in far]
        hessian = gram(spot, near, far, cols, stats, all_gains, gain[None, :])
    return (hessian[None], sections.reshape(1, M, TOK, WIDTH))


def solution(mesh):
    return jax.shard_map(
        body,
        mesh=mesh,
        in_specs=(
            P(None, "dp", "tensor"),
            P("pipe", "tensor"),
            P("pipe", "tensor", None, None),
            P("pipe", "tensor", None),
        ),
        out_specs=(P("pipe", "dp", "tensor"), P("pipe", None, "dp", "tensor")),
        check_vma=False,
    )
```

```python
import jax
import jax.numpy as jnp
from jax import lax
from jax.experimental import pallas as pl
from jax.experimental.pallas import tpu as pltpu
from jax.sharding import PartitionSpec as P

D = 12288
BLOCK = 64
KEEP = 48
M = 4
TOK = 64
ROWS = M * TOK
DP = 4
TENSOR = 16
WIDTH = D // TENSOR
QUARTER = D // DP
EPSILON = 1e-05
LANES = 128
SPAN = 256
CHUNK = 64
MIB = 1024 * 1024
VMEM_LIMIT = 61 * MIB
NEAR = [(dz, dy) for dz in range(2) for dy in range(4)]
ANY = pl.BlockSpec(memory_space=pl.ANY)
VMEM = pl.BlockSpec(memory_space=pltpu.VMEM)
SMEM = pl.BlockSpec(memory_space=pltpu.SMEM)


def build_kernel(rows_ref, blocks_ref, dense_ref):
    group = pl.program_id(0)

    @pl.loop(0, D // SPAN)
    def _(chunk):
        dense_ref[0, pl.ds(pl.multiple_of(chunk * SPAN, SPAN), SPAN), :] = jnp.zeros((SPAN, SPAN), jnp.bfloat16)

    per = SPAN // BLOCK

    @pl.loop(0, KEEP, unroll=4)
    def _(kept):
        for part in range(per):
            first = pl.multiple_of(rows_ref[per * group + part, kept] * BLOCK, BLOCK)
            dense_ref[0, pl.ds(first, BLOCK), part * BLOCK:(part + 1) * BLOCK] = blocks_ref[part, kept]


def build_dense(values, rows_index):
    blocks = values.reshape(WIDTH // BLOCK, KEEP, BLOCK, BLOCK)
    per = SPAN // BLOCK
    return pl.pallas_call(
        build_kernel,
        grid_spec=pltpu.PrefetchScalarGridSpec(
            num_scalar_prefetch=1,
            grid=(WIDTH // SPAN,),
            in_specs=[pl.BlockSpec((per, KEEP, BLOCK, BLOCK), lambda group, rows: (group, 0, 0, 0))],
            out_specs=pl.BlockSpec((1, D, SPAN), lambda group, rows: (group, 0, 0)),
        ),
        out_shape=jax.ShapeDtypeStruct((WIDTH // SPAN, D, SPAN), jnp.bfloat16),
        compiler_params=pltpu.CompilerParams(vmem_limit_bytes=VMEM_LIMIT),
        cost_estimate=pl.CostEstimate(flops=0, bytes_accessed=32 * MIB, transcendentals=0),
        name="build_dense",
    )(rows_index, blocks)


def start_pieces(pieces, refs, rows, sems):
    for array, start, count, position, into in pieces:
        pltpu.make_async_copy(
            refs[array].at[pl.ds(start, count)], rows.at[position, pl.ds(into, count)], sems.at[position]
        ).start()


def wait_block(rows, sems, position):
    pltpu.make_async_copy(rows.at[position], rows.at[position], sems.at[position]).wait()


def spread(column, means, span):
    means[span] = jnp.broadcast_to(column, (ROWS, LANES))


def block_at(spot_ref, position):
    z = lax.rem(spot_ref[1] + lax.rem(position // 4, 2), 2)
    y = lax.rem(spot_ref[2] + lax.rem(position, 4), 4)
    core = lax.rem(spot_ref[3] + position // len(NEAR), 2)
    return z * 8 + y * 2 + core


def layer_kernel(pieces, count, straight, spot_ref, weight_ref, gains_ref, own_ref, *refs):
    if not straight:
        earlier_ref, refs = refs[0], refs[1:]
    sources, (out_ref, stats_ref, rows, weight, total, means, scales, sems, weight_sems) = refs[:count], refs[count:]

    def place(position):
        return position if straight else block_at(spot_ref, position)

    def weight_copy(position):
        span = pl.ds(pl.multiple_of(place(position) * WIDTH, WIDTH), WIDTH)
        into = pl.ds(pl.multiple_of(position * WIDTH, WIDTH), WIDTH)
        return pltpu.make_async_copy(weight_ref.at[:, span], weight.at[:, into], weight_sems.at[position])

    start_pieces(pieces, sources, rows, sems)
    weight_copy(0).start()
    weight_copy(1).start()
    means[...] = jnp.zeros_like(means)
    scales[...] = jnp.zeros_like(scales)
    total[...] = own_ref[...].astype(jnp.float32)
    @pl.loop(0, TENSOR // 2)
    def _(pair):
        for position in (2 * pair, 2 * pair + 1):
            wait_block(rows, sems, position)
            for chunk in range(0, ROWS, CHUNK):
                span = slice(chunk, chunk + CHUNK)
                added = jnp.zeros((CHUNK, LANES), jnp.float32)
                squared = added
                for part in range(WIDTH // LANES):
                    values = rows[position, span, part * LANES:(part + 1) * LANES].astype(jnp.float32)
                    added = added + values
                    squared = squared + values * values
                means[span] += added
                scales[span] += squared

        @pl.when(pair + 2 < TENSOR // 2)
        def _():
            weight_copy(pair + 2).start()

    mean = jnp.sum(means[...], axis=1, keepdims=True) / D
    square = jnp.sum(scales[...], axis=1, keepdims=True) / D
    scale = lax.rsqrt(square - mean * mean + EPSILON)
    lane = lax.broadcasted_iota(jnp.int32, (ROWS, LANES), 1)
    stats_ref[...] = jnp.transpose(jnp.where(lane == 0, mean, scale))[:8]
    spread(mean, means, slice(0, ROWS))
    spread(scale, scales, slice(0, ROWS))

    def normalise(position):
        gain = gains_ref[place(position)]
        for chunk in range(0, ROWS, CHUNK):
            span = slice(chunk, chunk + CHUNK)
            for part in range(WIDTH // LANES):
                lanes = slice(part * LANES, (part + 1) * LANES)
                values = rows[position, span, lanes].astype(jnp.float32)
                scaled = (values - means[span]) * scales[span] * gain[:, lanes]
                rows[position, span, lanes] = scaled.astype(jnp.bfloat16)

    normalise(0)
    normalise(1)

    @pl.loop(0, TENSOR // 2)
    def _(pair):
        position = 2 * pair
        for later in range(2):

            @pl.when(position + TENSOR // 2 + later < TENSOR)
            def _():
                weight_copy(position + TENSOR // 2 + later).start()

        weight_copy(position).wait()
        weight_copy(position + 1).wait()
        left = jnp.concatenate([rows[position], rows[position + 1]], axis=1)
        span = pl.ds(pl.multiple_of(position * WIDTH, 2 * WIDTH), 2 * WIDTH)
        for group in range(WIDTH // SPAN):
            lanes = slice(group * SPAN, (group + 1) * SPAN)
            total[:, lanes] += jnp.dot(left, weight[group, span], preferred_element_type=jnp.float32)

        @pl.when(position + 2 < TENSOR)
        def _():
            normalise(position + 2)
            normalise(position + 3)

    out_ref[...] = total[...].astype(jnp.bfloat16)
    if not straight:

        @pl.when(spot_ref[4] == 0)
        def _():
            out_ref[...] = earlier_ref[...]


def in_hbm(arrays):
    return [pltpu.with_memory_space_constraint(array, pltpu.HBM) for array in arrays]


def layer(spot, gathered, pieces, weight, gains, own, earlier=None):
    count, straight = len(gathered), earlier is None
    return pl.pallas_call(
        lambda *refs: layer_kernel(pieces, count, straight, *refs),
        in_specs=[SMEM, ANY, VMEM, VMEM] + [VMEM] * (not straight) + [ANY] * count,
        out_specs=[VMEM, VMEM],
        out_shape=[
            jax.ShapeDtypeStruct((ROWS, WIDTH), jnp.bfloat16),
            jax.ShapeDtypeStruct((8, ROWS), jnp.float32),
        ],
        scratch_shapes=[
            pltpu.VMEM((TENSOR, ROWS, WIDTH), jnp.bfloat16),
            pltpu.VMEM((WIDTH // SPAN, D, SPAN), jnp.bfloat16),
            pltpu.VMEM((ROWS, WIDTH), jnp.float32),
            pltpu.VMEM((ROWS, LANES), jnp.float32),
            pltpu.VMEM((ROWS, LANES), jnp.float32),
            pltpu.SemaphoreType.DMA((TENSOR,)),
            pltpu.SemaphoreType.DMA((TENSOR,)),
        ],
        compiler_params=pltpu.CompilerParams(vmem_limit_bytes=VMEM_LIMIT),
        cost_estimate=pl.CostEstimate(flops=2 * ROWS * D * WIDTH, bytes_accessed=2 * D * (WIDTH + ROWS), transcendentals=ROWS),
        name="layer",
    )(spot, *in_hbm([weight]), gains, own, *([] if straight else [earlier]), *in_hbm(gathered))


PIECE = 384
PER = WIDTH // PIECE
HALF = TENSOR // DP // 2
CLASSES = [(side, half) for side in range(2) for half in range(HALF)]


def half_at(spot_ref, step):
    return spot_ref[1] if step == 2 else lax.rem(spot_ref[2], 2)


def pick_kernel(pieces, count, spot_ref, *refs):
    sources, picked, sems = refs[:count], refs[count + 1:-1], refs[-1]
    jobs = [(0, 0, 0), (0, 1, 1)] + [(step, half_at(spot_ref, step), 0) for step in range(1, DP)]
    for job, (step, half, into) in enumerate(jobs):
        target = lax.rem(spot_ref[0] + step, DP)
        dz = lax.rem(target // 2 + 2 - spot_ref[1], 2)
        dy = lax.rem(lax.rem(target, 2) * 2 + half + 4 - spot_ref[2], 4)
        for position in range(len(NEAR)):

            @pl.when(dz * 4 + dy == position)
            def _():
                for array, start, size, at, row in pieces:
                    if at == position:
                        pltpu.make_async_copy(
                            sources[array].at[pl.ds(start, size)],
                            picked[step].at[pl.ds(into * ROWS + row, size)],
                            sems.at[job],
                        ).start()

    for job, (step, _, into) in enumerate(jobs):
        block = picked[step].at[pl.ds(into * ROWS, ROWS)]
        pltpu.make_async_copy(block, block, sems.at[job]).wait()


def pick(spot, gathered, pieces, before):
    count = len(gathered)
    return pl.pallas_call(
        lambda *refs: pick_kernel(pieces, count, *refs),
        in_specs=[SMEM] + [ANY] * (count + 1),
        out_specs=[VMEM] * DP,
        out_shape=[jax.ShapeDtypeStruct((rows, WIDTH), jnp.bfloat16) for rows in [HALF * ROWS] + [ROWS] * (DP - 1)],
        scratch_shapes=[pltpu.SemaphoreType.DMA((DP + 1,))],
        compiler_params=pltpu.CompilerParams(vmem_limit_bytes=VMEM_LIMIT),
        cost_estimate=pl.CostEstimate(flops=0, bytes_accessed=4 * (DP + 1) * ROWS * WIDTH, transcendentals=0),
        name="pick",
    )(spot, *in_hbm(gathered), before)


def after(values, others):
    count = len(values)
    return pl.pallas_call(
        lambda *refs: None,
        in_specs=[ANY] * (count + len(others)),
        out_specs=[ANY] * count,
        out_shape=[jax.ShapeDtypeStruct(value.shape, value.dtype) for value in values],
        input_output_aliases={place: place for place in range(count)},
        name="after",
    )(*in_hbm(values), *others)


def gram_kernel(spot_ref, *refs):
    near, far, refs = refs[:2 * DP], refs[2 * DP:4 * DP - 2], refs[4 * DP - 2:]
    stats_refs, refs = refs[:DP], refs[DP:]
    cols_ref, gains_ref, col_gain_ref, out_ref, rows, given, cols, means, scales, left, result, sems, row_sems, col_sem = refs

    def block_of(group):
        return lax.rem(spot_ref[3] + group // HALF, 2) + 2 * lax.rem(group, HALF)

    def row_copy(source, group, part):
        return pltpu.make_async_copy(source, rows.at[group, part], row_sems.at[group, part])

    def start_rows(side):
        for half in range(HALF):
            row_copy(near[side * DP].at[pl.ds(half * ROWS, ROWS)], side * HALF + half, 0).start()
        for part in range(1, DP):
            half = half_at(spot_ref, part)
            row_copy(near[side * DP + part], side * HALF + half, part).start()
            row_copy(far[side * (DP - 1) + part - 1], side * HALF + 1 - half, part).start()

    columns = pltpu.make_async_copy(cols_ref, given, col_sem)
    columns.start()
    start_rows(0)
    for part in range(DP):
        span = slice(part * ROWS, (part + 1) * ROWS)
        means[span] = jnp.transpose(jnp.broadcast_to(stats_refs[part][0:1], (LANES, ROWS)))
        scales[span] = jnp.transpose(jnp.broadcast_to(stats_refs[part][1:2], (LANES, ROWS)))
    columns.wait()
    for part in range(DP):
        for chunk in range(0, ROWS, CHUNK):
            span = slice(part * ROWS + chunk, part * ROWS + chunk + CHUNK)
            for lane in range(WIDTH // LANES):
                lanes = slice(lane * LANES, (lane + 1) * LANES)
                values = given[lax.rem(spot_ref[0] + DP - part, DP), chunk:chunk + CHUNK, lanes].astype(jnp.float32)
                scaled = (values - means[span]) * scales[span] * col_gain_ref[:, lanes]
                cols[span, lanes] = scaled.astype(jnp.bfloat16)

    def normalise(group, slot):
        if slot == 0:
            for part in range(DP):
                row_copy(rows.at[group, part], group, part).wait()
        gain = gains_ref[spot_ref[0] * (TENSOR // DP) + block_of(group)]
        for part in range(DP):
            for chunk in range(0, ROWS, CHUNK):
                span = slice(part * ROWS + chunk, part * ROWS + chunk + CHUNK)
                for lane in range(PIECE // LANES):
                    first = slot * PIECE + lane * LANES
                    from_lanes = slice(first, first + LANES)
                    values = rows[group, part, chunk:chunk + CHUNK, from_lanes].astype(jnp.float32)
                    scaled = (values - means[span]) * scales[span] * gain[:, from_lanes]
                    left[slot, span, lane * LANES:(lane + 1) * LANES] = scaled.astype(jnp.bfloat16)

    def store(group, slot):
        row = pl.multiple_of(block_of(group) * WIDTH + slot * PIECE, PIECE)
        return pltpu.make_async_copy(result.at[slot], out_ref.at[pl.ds(row, PIECE)], sems.at[slot])

    normalise(0, 0)
    start_rows(1)

    for group in range(len(CLASSES)):
        for slot in range(PER):
            product = lax.dot_general(
                left[slot], cols[...], (((0,), (0,)), ((), ())), preferred_element_type=jnp.float32
            )
            if group > 0:
                store(group - 1, slot).wait()
            result[slot] = product * (2.0 / (DP * ROWS))
            store(group, slot).start()
            if slot + 1 < PER:
                normalise(group, slot + 1)
            elif group + 1 < len(CLASSES):
                normalise(group + 1, 0)

    for slot in range(PER):
        store(len(CLASSES) - 1, slot).wait()


def gram(spot, near, far, cols, stats, gains, col_gain):
    return pl.pallas_call(
        gram_kernel,
        in_specs=[SMEM] + [ANY] * (4 * DP - 2) + [VMEM] * DP + [ANY, VMEM, VMEM],
        out_specs=ANY,
        out_shape=jax.ShapeDtypeStruct((QUARTER, WIDTH), jnp.float32),
        scratch_shapes=[
            pltpu.VMEM((len(CLASSES), DP, ROWS, WIDTH), jnp.bfloat16),
            pltpu.VMEM((DP, ROWS, WIDTH), jnp.bfloat16),
            pltpu.VMEM((DP * ROWS, WIDTH), jnp.bfloat16),
            pltpu.VMEM((DP * ROWS, LANES), jnp.float32),
            pltpu.VMEM((DP * ROWS, LANES), jnp.float32),
            pltpu.VMEM((2, DP * ROWS, PIECE), jnp.bfloat16),
            pltpu.VMEM((2, PIECE, WIDTH), jnp.float32),
            pltpu.SemaphoreType.DMA((2,)),
            pltpu.SemaphoreType.DMA((len(CLASSES), DP)),
            pltpu.SemaphoreType.DMA(()),
        ],
        compiler_params=pltpu.CompilerParams(vmem_limit_bytes=VMEM_LIMIT),
        cost_estimate=pl.CostEstimate(
            flops=2 * DP * ROWS * QUARTER * WIDTH, bytes_accessed=4 * QUARTER * WIDTH + 2 * DP * ROWS * (QUARTER + WIDTH), transcendentals=0
        ),
        name="gram",
    )(spot, *near, *far, *stats, *in_hbm([cols]), gains, col_gain)


def along_dp(value, step):
    return lax.ppermute(value, "dp", [(source, (source + step) % DP) for source in range(DP)])


def gather_dp(value):
    return [value] + [along_dp(value, step) for step in range(1, DP)]


def tensor_at(z, y, core):
    return (z % 2) * 8 + (y % 4) * 2 + core % 2


def shift(value, z, y, core):
    pairs = [
        (tensor_at(a, b, c), tensor_at(a + z, b + y, c + core)) for a in range(2) for b in range(4) for c in range(2)
    ]
    return lax.ppermute(value, "tensor", pairs)


def share(value, step):
    pairs = []
    for z in range(2):
        for y in range(4):
            for core in range(2):
                to = {1: (z, y ^ 1), 2: (1 - z, y), 3: (z, 3 - y)}[step]
                pairs.append((tensor_at(z, y, core), tensor_at(*to, core)))
    return lax.ppermute(value, "tensor", pairs)


def gather_near(value):
    rows = value.shape[0]
    cut, cut2 = rows * 3 // 8, rows * 11 // 16
    up, down, over = shift(value, 0, 1, 0), shift(value, 0, -1, 0), shift(value, 1, 0, 0)
    up2, over_up, over_down = shift(up, 0, 1, 0), shift(up, 1, 0, 0), shift(over, 0, -1, 0)
    far = [
        shift(up2[:cut], 1, 0, 0),
        shift(over_up[cut:cut2], 0, 1, 0),
        shift(over_down[cut2:], 0, -1, 0),
    ]
    mine = [value, down, up2, up, over, over_down, over_up] + far
    theirs = [shift(array, 0, 0, 1) for array in mine]
    pieces = []
    for side in range(2):
        at, pos = side * len(mine), side * len(NEAR)
        pieces += [(at + array, 0, rows, pos + position, 0) for array, position in enumerate([0, 1, 2, 3, 4, 5, 7])]
        pieces += [
            (at + 7, 0, cut, pos + 6, 0),
            (at + 8, 0, cut2 - cut, pos + 6, cut),
            (at + 9, 0, rows - cut2, pos + 6, cut2),
        ]
    return mine + theirs, pieces


def body(activations, gains, block_values, block_rows):
    first = lax.axis_index("pipe") == 0
    quarter = lax.axis_index("dp")
    here = lax.axis_index("tensor")
    gain = gains[0]
    own = activations.reshape(ROWS, WIDTH)
    with jax.named_scope("rows_first"):
        gathered = lax.all_gather(own, "tensor", axis=0, tiled=True)
    with jax.named_scope("gains"):
        all_gains = lax.all_to_all(jnp.broadcast_to(gain[None, :], (TENSOR, WIDTH)), "tensor", 0, 0, tiled=True)
        all_gains = all_gains[:, None, :]
    with jax.named_scope("weight"):
        weight = build_dense(block_values[0], block_rows[0])
    spot = jnp.stack([quarter, here // 8, here // 2 % 4, here % 2, lax.axis_index("pipe")]).astype(jnp.int32)
    with jax.named_scope("layer_first"):
        pieces = [(0, block * ROWS, ROWS, block, 0) for block in range(TENSOR)]
        updated_first, _ = layer(spot, [gathered], pieces, weight, all_gains, own)
    with jax.named_scope("hand_over"):
        received = lax.ppermute(updated_first, "pipe", [(0, 1)])
    stream = jnp.where(first, own, received)
    with jax.named_scope("columns"):
        cols = lax.all_gather(jnp.where(first, own, 0) + received, "dp", axis=0)
    with jax.named_scope("rows_second"):
        arrays, pieces = gather_near(stream)
    with jax.named_scope("hessian_rows"):
        mine = len(arrays) // 2
        picked = pick(spot, arrays[:mine], [piece for piece in pieces if piece[0] < mine], cols)
        rows = [along_dp(picked[step], step) for step in range(1, DP)]
    with jax.named_scope("layer_second"):
        sections, stats = layer(spot, arrays, pieces, weight, all_gains, stream, updated_first)
        stats = gather_dp(stats)
    with jax.named_scope("hessian"):
        near = [picked[0], *after(rows, [stats[0]])]
        far = [share(value, step) for step, value in enumerate(near) if step > 0]
        far[1:2] = after([far[1]], stats[1:])
        near += [shift(value, 0, 0, 1) for value in near]
        far += [shift(value, 0, 0, 1) for value in far]
        hessian = gram(spot, near, far, cols, stats, all_gains, gain[None, :])
    return (hessian[None], sections.reshape(1, M, TOK, WIDTH))


def solution(mesh):
    return jax.shard_map(
        body,
        mesh=mesh,
        in_specs=(
            P(None, "dp", "tensor"),
            P("pipe", "tensor"),
            P("pipe", "tensor", None, None),
            P("pipe", "tensor", None),
        ),
        out_specs=(P("pipe", "dp", "tensor"), P("pipe", None, "dp", "tensor")),
        check_vma=False,
    )
```
